256 devices in a mesh: span: 16 (over z_lo, x), chord: 16 (over y, z_hi, core).
Axes of the slice: x: 4, y: 4, z: 8 (z_hi: 2, z_lo: 4; z = z_hi * 4 + z_lo), core: 2. Of those that a mesh axis runs over, the one named last changes fastest.
Arguments:
- node_coords: float32 [3, 256, 256, 256], P(None, 'span', 'chord')
- primitives: float32 [5, 256, 256, 256], P(None, 'span', 'chord')
- control_points: float32 [3, 256, 64], P(None, ('span', 'chord'))
- coefficients: float32 [3, 256, 64], P(None, ('span', 'chord')), may hold values from -4 to 4
- support_tiles: int32 [16, 16, 6], P('span', 'chord'), may hold values from 0 to 255, as said below
- support_counts: int32 [16, 16], P('span', 'chord'), may hold values from 1 to 6, as said below
Outputs:
- grid_motion: float32 [3, 256, 256, 256], P(None, 'span', 'chord')
- section_state: float32 [5, 256, 256, 256], P(None, 'span', 'chord')
The draws below stay inside these ranges and needn't reach their ends.
Inputs may be any that keep to these rules, and one draw needn't show every extreme that they name: `support_tiles`: tile t lies in span block t // 16 and chord block t % 16; the first support_counts entries of a block's list are distinct tiles whose span and chord block differ from the block's own by at most one; later entries are unused. `support_counts`: some block uses all 6 slots.
All inputs are finite; a program needn't handle non-finite values.
Results may differ from the reference program's by a relative error of at most 0.0003.
Values sent between devices are 32-bit elements; how exact they have to be, the bound alone decides.
A program may use at most 64 MiB of HBM per device.

```python
import jax
import jax.numpy as jnp
from jax import lax

SPAN_DEV = 16
CHORD_DEV = 16
NORMAL = 256
CP_DEV = 64
S_MAX = 6
RADIUS = 12
NI = 256
NJ = 256
TILES = 256
N_SPAN = 16
N_CHORD = 16


def support_layout(key):
    key = jax.random.fold_in(key, 40)
    first_key, second_key, third_key, fourth_key, fifth_key = jax.random.split(key, 5)
    offsets = jnp.arange(9)
    span_shift = offsets // 3 - 1
    chord_shift = offsets % 3 - 1
    block_span = jnp.arange(N_SPAN)[:, None, None]
    block_chord = jnp.arange(N_CHORD)[None, :, None]
    target_span = block_span + span_shift[None, None, :]
    target_chord = block_chord + chord_shift[None, None, :]
    inside = (target_span >= 0) & (target_span < N_SPAN) & (target_chord >= 0) & (target_chord < N_CHORD)
    scores = jax.random.randint(first_key, (N_SPAN, N_CHORD, 9), 0, 1000) * 16 + offsets[None, None, :]
    scores = scores + jnp.where(inside, 0, 100000)
    order = jnp.argsort(scores, axis=-1)
    targets = target_span * N_CHORD + target_chord
    chosen = jnp.take_along_axis(targets, order, axis=-1)[..., :S_MAX]
    inside_count = jnp.sum(inside.astype(jnp.int32), -1)
    first_roll = jax.random.randint(second_key, (N_SPAN, N_CHORD), 0, S_MAX)
    second_roll = jax.random.randint(third_key, (N_SPAN, N_CHORD), 0, S_MAX)
    drawn = 1 + first_roll * second_roll // (S_MAX - 1)
    pick_span = jax.random.randint(fourth_key, (), 1, N_SPAN - 1)
    pick_chord = jax.random.randint(fifth_key, (), 1, N_CHORD - 1)
    chosen_block = (block_span[..., 0] == pick_span) & (block_chord[..., 0] == pick_chord)
    drawn = jnp.where(chosen_block, S_MAX, drawn)
    counts = jnp.minimum(drawn, inside_count)
    own_tile = block_span * N_CHORD + block_chord
    slots = jnp.arange(S_MAX)[None, None, :]
    chosen = jnp.where(slots < counts[..., None], chosen, own_tile)
    return (chosen.astype(jnp.int32), counts.astype(jnp.int32))


def draw_support_tiles(key, part):
    return support_layout(key)[0]


def draw_support_counts(key, part):
    return support_layout(key)[1]


def draw_node_coords(key, part):
    key = jax.random.fold_in(key, 1)
    shape = (NI, NJ, NORMAL)
    span_pos = jnp.broadcast_to(jnp.arange(NI, dtype=jnp.float32)[:, None, None], shape)
    chord_pos = jnp.broadcast_to(jnp.arange(NJ, dtype=jnp.float32)[None, :, None], shape)
    normal_pos = jnp.broadcast_to(jnp.arange(NORMAL, dtype=jnp.float32)[None, None, :], shape)
    spread = 0.2
    jitter = jax.random.uniform(key, (3, NI, NJ, NORMAL), jnp.float32, -spread, spread)
    return jnp.stack([span_pos, chord_pos, normal_pos], 0) + jitter


def draw_primitives(key, part):
    key = jax.random.fold_in(key, 2)
    first_key, second_key, third_key = jax.random.split(key, 3)
    shape = (NI, NJ, NORMAL)
    pressure = jnp.exp(jax.random.uniform(third_key, shape, jnp.float32, -0.69, 0.69))
    density = jnp.exp(jax.random.uniform(first_key, shape, jnp.float32, -0.69, 0.69))
    velocity = 0.5 * jax.random.normal(second_key, (3, NI, NJ, NORMAL), jnp.float32)
    return jnp.concatenate([density[None], velocity, pressure[None]], 0)


def draw_control_points(key, part):
    key = jax.random.fold_in(key, 3)
    tiles = jnp.arange(N_SPAN * N_CHORD)
    span_block = (tiles // N_CHORD).astype(jnp.float32)[:, None]
    chord_block = (tiles % N_CHORD).astype(jnp.float32)[:, None]
    uniform = jax.random.uniform(key, (3, N_SPAN * N_CHORD, CP_DEV), jnp.float32)
    span_pos = (span_block + uniform[0]) * SPAN_DEV
    chord_pos = (chord_block + uniform[1]) * CHORD_DEV
    normal_pos = uniform[2] * NORMAL
    return jnp.stack([span_pos, chord_pos, normal_pos], 0)


def shard_levels(rng, extent, pieces, low, largest):
    def one(axis_at, blocks):
        heights = jax.random.uniform(jax.random.fold_in(jax.random.fold_in(rng, 6), axis_at), (blocks,), jnp.float32, low / len(pieces), largest / len(pieces))
        return jnp.repeat(jnp.exp(heights), extent[axis_at] // blocks).reshape((-1,) + (1,) * (len(extent) - axis_at - 1))

    gain = one(*pieces[0])
    for cut in pieces[1:]:
        gain = gain * one(*cut)
    return gain


def scatter_about(rng, shape, width, reach, cuts=(), kind=jnp.bfloat16):
    entries = jax.random.normal(rng, shape, jnp.float32) * width
    if len(cuts) > 0:
        entries = shard_levels(rng, shape, cuts, -0.22, 0.18) * entries
    return jnp.clip(entries, min=-reach, max=reach).astype(kind)


def setup_inputs(seed: int = 0) -> dict:
    key_list = jax.random.split(jax.random.key(seed), 7)
    node_coords = draw_node_coords(jax.random.fold_in(key_list[6], 71), 0)
    primitives = draw_primitives(jax.random.fold_in(key_list[6], 71), 0)
    control_points = draw_control_points(jax.random.fold_in(key_list[6], 71), 0)
    coefficients = scatter_about(key_list[3], (3, TILES, CP_DEV), 0.3, 4.0, ((1, 256),), jnp.float32)
    support_tiles = draw_support_tiles(jax.random.fold_in(key_list[6], 71), 0)
    support_counts = draw_support_counts(jax.random.fold_in(key_list[6], 71), 0)
    return dict(node_coords=node_coords, primitives=primitives, control_points=control_points, coefficients=coefficients, support_tiles=support_tiles, support_counts=support_counts)


GAMMA_GAS = 1.4
SECTION_BETA = 0.2

def wendland(squared):
    ratio = jnp.sqrt(squared) / RADIUS
    remain = jnp.maximum(1.0 - ratio, 0.0)
    fourth = remain * remain * (remain * remain)
    return fourth * (4.0 * ratio + 1.0)

def tile_motion(nodes_flat, tile_points, tile_coef):
    first = nodes_flat[0][None, :] - tile_points[0][:, None]
    second = nodes_flat[1][None, :] - tile_points[1][:, None]
    third = nodes_flat[2][None, :] - tile_points[2][:, None]
    weights = wendland(first * first + second * second + third * third)
    return jnp.dot(tile_coef, weights, precision=lax.Precision.HIGHEST, preferred_element_type=jnp.float32)

def conserved(states):
    density = states[0]
    velocity = states[1:4]
    pressure = states[4]
    kinetic = 0.5 * density * lax.optimization_barrier(jnp.sum(velocity * velocity, 0))
    energy = pressure / (GAMMA_GAS - 1.0) + kinetic
    return jnp.concatenate([density[None], density[None] * velocity, energy[None]], 0)

def face_flux(left_coords, right_coords, left_speed, right_speed, left_state, right_state):
    edge_vec = right_coords - left_coords
    normal = edge_vec / lax.optimization_barrier(jnp.sum(edge_vec * edge_vec, 0))
    frame_speed = lax.optimization_barrier(jnp.sum(0.5 * (left_speed + right_speed) * normal, 0))
    magnitude = jnp.sqrt(lax.optimization_barrier(jnp.sum(normal * normal, 0)))

    def one_side(states):
        velocity = states[1:4]
        pressure = states[4]
        normal_speed = lax.optimization_barrier(jnp.sum(velocity * normal, 0))
        relative = normal_speed - frame_speed
        amounts = conserved(states)
        extra = jnp.concatenate([jnp.zeros_like(pressure)[None], pressure[None] * normal, (pressure * normal_speed)[None]], 0)
        fluxes = amounts * relative[None] + extra
        signal = jnp.abs(relative) + jnp.sqrt(GAMMA_GAS * pressure / states[0]) * magnitude
        return (amounts, fluxes, signal)
    left_amounts, left_fluxes, left_signal = one_side(left_state)
    right_amounts, right_fluxes, right_signal = one_side(right_state)
    return 0.5 * (left_fluxes + right_fluxes) - 0.5 * jnp.maximum(left_signal, right_signal)[None] * (right_amounts - left_amounts)

def block_motion(nodes_flat, tiles_row, count, control_points, coefficients):

    def add_tile(slot, total):
        tile = lax.dynamic_index_in_dim(tiles_row, slot, 0, keepdims=False)
        tile_points = lax.dynamic_index_in_dim(control_points, tile, 1, keepdims=False)
        tile_coef = lax.dynamic_index_in_dim(coefficients, tile, 1, keepdims=False)
        return total + tile_motion(nodes_flat, tile_points, tile_coef)
    return lax.fori_loop(0, count, add_tile, jnp.zeros(nodes_flat.shape, jnp.float32))

def slab_section(row_index, node_coords, motion, primitives):
    rows = jnp.clip(row_index * SPAN_DEV - 1 + jnp.arange(SPAN_DEV + 2), 0, NI - 1).astype(jnp.int32)
    place = jnp.take(node_coords, rows, axis=1) + jnp.take(motion, rows, axis=1)
    speed = jnp.take(motion, rows, axis=1)
    states = jnp.take(primitives, rows, axis=1)
    span_flux = face_flux(place[:, :-1], place[:, 1:], speed[:, :-1], speed[:, 1:], states[:, :-1], states[:, 1:])
    faces = jnp.arange(SPAN_DEV + 1)
    keep = jnp.logical_not((row_index == 0) & (faces == 0) | (row_index == N_SPAN - 1) & (faces == SPAN_DEV))
    span_flux = jnp.where(keep[None, :, None, None], span_flux, 0.0)
    residual = span_flux[:, 1:] - span_flux[:, :-1]
    mid_place = place[:, 1:-1]
    mid_speed = speed[:, 1:-1]
    mid_states = states[:, 1:-1]
    chord_flux = face_flux(mid_place[:, :, :-1], mid_place[:, :, 1:], mid_speed[:, :, :-1], mid_speed[:, :, 1:], mid_states[:, :, :-1], mid_states[:, :, 1:])
    residual = residual + (jnp.pad(chord_flux, ((0, 0), (0, 0), (0, 1), (0, 0))) - jnp.pad(chord_flux, ((0, 0), (0, 0), (1, 0), (0, 0))))
    normal_flux = face_flux(mid_place[..., :-1], mid_place[..., 1:], mid_speed[..., :-1], mid_speed[..., 1:], mid_states[..., :-1], mid_states[..., 1:])
    residual = residual + (jnp.pad(normal_flux, ((0, 0), (0, 0), (0, 0), (0, 1))) - jnp.pad(normal_flux, ((0, 0), (0, 0), (0, 0), (1, 0))))
    return conserved(mid_states) - SECTION_BETA * residual

def reference(node_coords, primitives, control_points, coefficients, support_tiles, support_counts):
    blocks = node_coords.reshape(3, N_SPAN, SPAN_DEV, N_CHORD, CHORD_DEV, NORMAL)
    blocks = blocks.transpose(1, 3, 0, 2, 4, 5).reshape(N_SPAN * N_CHORD, 3, SPAN_DEV * CHORD_DEV * NORMAL)
    lists = support_tiles.reshape(N_SPAN * N_CHORD, S_MAX)
    counts = support_counts.reshape(N_SPAN * N_CHORD)

    def one_block(packed):
        return block_motion(packed[0], packed[1], packed[2], control_points, coefficients)
    moved = lax.map(one_block, (blocks, lists, counts))
    moved = moved.reshape(N_SPAN, N_CHORD, 3, SPAN_DEV, CHORD_DEV, NORMAL)
    grid_motion = moved.transpose(2, 0, 3, 1, 4, 5).reshape(3, NI, NJ, NORMAL)

    def one_slab(row_index):
        return slab_section(row_index, node_coords, grid_motion, primitives)
    slabs = lax.map(one_slab, jnp.arange(N_SPAN).astype(jnp.int32))
    section_state = slabs.transpose(1, 0, 2, 3, 4).reshape(5, NI, NJ, NORMAL)
    return (grid_motion, section_state)
```

```python
import jax
import jax.numpy as jnp
from jax import lax
from jax.experimental import pallas as pl
from jax.experimental.pallas import tpu as pltpu
from jax.sharding import PartitionSpec as P

RADIUS = 12
GAMMA_GAS = 1.4
SECTION_BETA = 0.2
SLOTS = 6
BATCH = 8
FAR = 3.0e38
REACH = 1.001
MESH = pl.DeviceIdType.MESH
AROUND = tuple((a, b) for a in (-1, 0, 1) for b in (-1, 0, 1) if (a, b) != (0, 0))
SIDES = ((-1, 0), (1, 0), (0, -1), (0, 1))


def peer(offset):
    spans, chords = lax.axis_size("span"), lax.axis_size("chord")
    return {
        "span": lax.rem(lax.axis_index("span") + offset[0] + spans, spans),
        "chord": lax.rem(lax.axis_index("chord") + offset[1] + chords, chords),
    }


def meet(offsets):
    barrier = pltpu.get_barrier_semaphore()
    for offset in offsets:
        pl.semaphore_signal(barrier, inc=1, device_id=peer(offset), device_id_type=MESH)
    return lambda: pl.semaphore_wait(barrier, len(offsets))


def gather_kernel(
    x_hbm,
    q_hbm,
    points_ref,
    coef_ref,
    tiles_ref,
    count_ref,
    xt_ref,
    sorted_ref,
    range_ref,
    rims_ref,
    x_v,
    q_v,
    own,
    window,
    stage,
    local_sems,
    send_sems,
    recv_sems,
):
    wait_all = meet(AROUND)
    get_x = pltpu.make_async_copy(x_hbm, x_v, local_sems.at[0])
    get_q = pltpu.make_async_copy(q_hbm, q_v, local_sems.at[1])
    get_x.start()
    get_q.start()

    scale = 1.0 / RADIUS
    own[...] = jnp.zeros_like(own)
    for half in range(2):
        lanes = pl.ds(64 * half, 64)
        own[0:3, lanes] = points_ref[:, 0, :] * scale
        own[3:6, lanes] = coef_ref[:, 0, :]
    wait_all()

    copies = []

    def send(src, dst, offset):
        at = len(copies)
        copy = pltpu.make_async_remote_copy(
            src_ref=src,
            dst_ref=dst,
            send_sem=send_sems.at[at],
            recv_sem=recv_sems.at[at],
            device_id=peer(offset),
            device_id_type=MESH,
        )
        copy.start()
        copies.append(copy)

    for a, b in AROUND:
        send(own, window.at[(1 - a) * 3 + 1 - b], (a, b))
    window[4] = own[...]

    length = x_v.shape[1]
    get_x.wait()
    get_q.wait()
    for side, row in ((2, 0), (3, length - 1)):
        stage[side, 0:3] = x_v[:, :, row, :]
        stage[side, 3:8] = q_v[:, :, row, :]
    for side, row in ((0, 0), (1, length - 1)):
        stage[side, 0:3] = x_v[:, row]
        stage[side, 3:8] = q_v[:, row]
    for side, offset in enumerate(SIDES):
        send(stage.at[side], rims_ref.at[side ^ 1], offset)

    low, high = [], []
    for k in range(3):
        low.append(jnp.min(jnp.min(x_v[k], axis=0), axis=0, keepdims=True) * scale)
        high.append(jnp.max(jnp.max(x_v[k], axis=0), axis=0, keepdims=True) * scale)
    for k in range(3):
        for h in range(2):
            for j in range(2):
                part = x_v[k, 8 * h : 8 * h + 8, :, 128 * j : 128 * j + 128]
                part = part.reshape(128, 128) * scale
                xt_ref[k, 128 * j : 128 * j + 128, 128 * h : 128 * h + 128] = part.T

    for copy in copies[:8]:
        copy.wait()
    span_at, chord_at = lax.axis_index("span"), lax.axis_index("chord")
    chords = lax.axis_size("chord")
    count = count_ref[0, 0]
    lane = lax.broadcasted_iota(jnp.int32, (8, 128), 1)
    row_at = lax.broadcasted_iota(jnp.int32, (8, 128), 0)

    def picked(slot):
        tile = tiles_ref[0, 0, slot]
        at = (tile // chords - span_at + 1) * 3 + (tile % chords - chord_at + 1)
        return window[jnp.clip(at, 0, 8)]

    box = [
        (jnp.min(low[k], axis=1, keepdims=True) - REACH, jnp.max(high[k], axis=1, keepdims=True) + REACH)
        for k in range(2)
    ]
    values, keys = [], []
    for pair in range(SLOTS // 2):
        value = jnp.where(lane < 64, picked(2 * pair), picked(2 * pair + 1))
        used = jnp.where(lane < 64, 2 * pair, 2 * pair + 1) < count
        value = jnp.where((row_at >= 3) & jnp.logical_not(used), 0.0, value)
        keep = used[0:1]
        for k in range(2):
            keep = keep & (value[k : k + 1] > box[k][0]) & (value[k : k + 1] < box[k][1])
        keys.append(jnp.where(keep, value[2:3], FAR))
        values.append(value)

    columns = [jnp.broadcast_to(key, (128, 128)).T for key in keys]
    big_lane = lax.broadcasted_iota(jnp.int32, (128, 128), 1)
    big_row = lax.broadcasted_iota(jnp.int32, (128, 128), 0)
    groups = len(keys)
    total = jnp.zeros((32, 128 * groups), jnp.float32)
    for j in range(groups):
        ahead = jnp.zeros((128, 128), jnp.float32)
        for i in range(groups):
            if i < j:
                before = keys[i] <= columns[j]
            elif i > j:
                before = keys[i] < columns[j]
            else:
                before = (keys[i] < columns[j]) | ((keys[i] == columns[j]) & (big_lane < big_row))
            ahead = ahead + jnp.where(before, 1.0, 0.0)
        rank = jnp.sum(ahead, axis=1, keepdims=True).astype(jnp.int32)
        place = jnp.concatenate(
            [jnp.where(rank == big_lane + 128 * i, 1.0, 0.0) for i in range(groups)], axis=1
        ).astype(jnp.bfloat16)
        first = values[j].astype(jnp.bfloat16).astype(jnp.float32)
        rest = values[j] - first
        second = rest.astype(jnp.bfloat16).astype(jnp.float32)
        third = rest - second
        parts = jnp.concatenate([first, second, third, jnp.zeros_like(third)], axis=0)
        total = total + jnp.dot(
            parts.astype(jnp.bfloat16), place, preferred_element_type=jnp.float32
        )
    sorted_ref[:, 0 : 128 * groups] = total[0:8] + total[8:16] + total[16:24]
    sorted_ref[:, 128 * groups :] = jnp.zeros((8, 128), jnp.float32)

    depth = x_v.shape[3]
    z_low = jnp.broadcast_to(low[2], (8, depth))
    z_high = jnp.broadcast_to(high[2], (8, depth))
    for shift in (1, 2, 4):
        z_low = jnp.minimum(z_low, pltpu.roll(z_low, depth - shift, axis=1))
        z_high = jnp.maximum(z_high, pltpu.roll(z_high, depth - shift, axis=1))
    for at, (edge, test) in enumerate(
        ((z_low - REACH, jnp.less), (z_high + REACH, jnp.less_equal))
    ):
        for h in range(depth // 128):
            part = edge[0:1, 128 * h : 128 * h + 128]
            found = sum(jnp.where(test(column, part), 1.0, 0.0) for column in columns)
            found = jnp.sum(found, axis=0, keepdims=True).astype(jnp.int32)
            range_ref[at : at + 1, 128 * h : 128 * h + 128] = found
    for copy in copies[8:]:
        copy.wait()


def gather(node_coords, primitives, control_points, coefficients, tiles, counts):
    depth = node_coords.shape[3]
    vmem = pl.BlockSpec(memory_space=pltpu.VMEM)
    smem = pl.BlockSpec(memory_space=pltpu.SMEM)
    anywhere = pl.BlockSpec(memory_space=pl.ANY)
    f32 = jnp.float32
    return pl.pallas_call(
        gather_kernel,
        out_shape=(
            jax.ShapeDtypeStruct((3, depth, 256), f32),
            jax.ShapeDtypeStruct((8, 64 * SLOTS + 128), f32),
            jax.ShapeDtypeStruct((8, depth), jnp.int32),
            jax.ShapeDtypeStruct((4, 8, 16, depth), f32),
        ),
        in_specs=[anywhere, anywhere, vmem, vmem, smem, smem],
        out_specs=(vmem, vmem, vmem, anywhere),
        scratch_shapes=[
            pltpu.VMEM(node_coords.shape, f32),
            pltpu.VMEM(primitives.shape, f32),
            pltpu.VMEM((8, 128), f32),
            pltpu.VMEM((9, 8, 128), f32),
            pltpu.VMEM((4, 8, 16, depth), f32),
            pltpu.SemaphoreType.DMA((2,)),
            pltpu.SemaphoreType.DMA((12,)),
            pltpu.SemaphoreType.DMA((12,)),
        ],
        compiler_params=pltpu.CompilerParams(
            collective_id=0, has_side_effects=True, vmem_limit_bytes=32 << 20
        ),
        name="gather",
    )(node_coords, primitives, control_points, coefficients, tiles, counts)


def motion_kernel(sorted_ref, range_ref, xt_ref, out_ref, mt_ref):
    depth = xt_ref.shape[1]

    def chunk(c, carry):
        rows = pl.ds(pl.multiple_of(c * 8, 8), 8)
        x, y, z = (xt_ref[k, rows, :] for k in range(3))
        start, stop = range_ref[0, c * 8], range_ref[1, c * 8]

        def step(i, total):
            total = list(total)
            base = start + i * BATCH
            for u in range(BATCH):
                at = base + u
                dx = x - sorted_ref[0, at]
                dy = y - sorted_ref[1, at]
                dz = z - sorted_ref[2, at]
                squared = jnp.maximum(dx * dx + dy * dy + dz * dz, 1e-30)
                ratio = squared * lax.rsqrt(squared)
                remain = jnp.maximum(1.0 - ratio, 0.0)
                second = remain * remain
                weight = second * second * (5.0 - 4.0 * remain)
                for k in range(3):
                    total[k] = total[k] + sorted_ref[3 + k, at] * weight
            return tuple(total)

        zero = jnp.zeros_like(x)
        total = lax.fori_loop(0, (stop - start + BATCH - 1) // BATCH, step, (zero, zero, zero))
        for k in range(3):
            mt_ref[k, rows, :] = total[k]
        return carry

    lax.fori_loop(0, depth // 8, chunk, 0)
    for k in range(3):
        for h in range(2):
            for j in range(2):
                part = mt_ref[k, 128 * j : 128 * j + 128, 128 * h : 128 * h + 128].T
                out_ref[k, 8 * h : 8 * h + 8, :, 128 * j : 128 * j + 128] = part.reshape(8, 16, 128)


def motion(points, ranges, coords_t, shape):
    vmem = pl.BlockSpec(memory_space=pltpu.VMEM)
    smem = pl.BlockSpec(memory_space=pltpu.SMEM)
    return pl.pallas_call(
        motion_kernel,
        out_shape=jax.ShapeDtypeStruct(shape, jnp.float32),
        in_specs=[smem, smem, vmem],
        out_specs=vmem,
        scratch_shapes=[pltpu.VMEM(coords_t.shape, jnp.float32)],
        compiler_params=pltpu.CompilerParams(vmem_limit_bytes=32 << 20),
        name="motion",
    )(points, ranges, coords_t)


def node_fields(coords, speed, state):
    rho, u, p = state[0], state[1:4], state[4]
    kinetic = 0.5 * rho * (u[0] * u[0] + u[1] * u[1] + u[2] * u[2])
    return dict(
        place=[a + b for a, b in zip(coords, speed)],
        speed=speed,
        u=u,
        p=p,
        amounts=[rho] + [rho * v for v in u] + [p / (GAMMA_GAS - 1.0) + kinetic],
        sound=jnp.sqrt(GAMMA_GAS * p / rho),
    )


def dot3(a, b):
    return a[0] * b[0] + a[1] * b[1] + a[2] * b[2]


def double_flux(left, right):
    edge = [b - a for a, b in zip(left["place"], right["place"])]
    magnitude = lax.rsqrt(dot3(edge, edge))
    inverse = magnitude * magnitude
    normal = [e * inverse for e in edge]
    frame = 0.5 * dot3([a + b for a, b in zip(left["speed"], right["speed"])], normal)
    left_un, right_un = dot3(left["u"], normal), dot3(right["u"], normal)
    left_rel, right_rel = left_un - frame, right_un - frame
    signal = jnp.maximum(
        jnp.abs(left_rel) + left["sound"] * magnitude,
        jnp.abs(right_rel) + right["sound"] * magnitude,
    )
    left_gain, right_gain = left_rel + signal, right_rel - signal
    flux = [a * left_gain + b * right_gain for a, b in zip(left["amounts"], right["amounts"])]
    pressure = left["p"] + right["p"]
    for k in range(3):
        flux[1 + k] = flux[1 + k] + pressure * normal[k]
    flux[4] = flux[4] + left["p"] * left_un + right["p"] * right_un
    return flux


def flux_kernel(
    x_ref,
    m_ref,
    q_ref,
    rims_ref,
    out_ref,
    stage,
    landed,
    send_sems,
    recv_sems,
):
    wait_all = meet(SIDES)
    length, chord_len, depth = x_ref.shape[1:]
    last = length - 1
    stage[0] = m_ref[:, 0]
    stage[1] = m_ref[:, last]
    stage[2] = m_ref[:, :, 0, :]
    stage[3] = m_ref[:, :, last, :]
    wait_all()
    copies = []
    for side, offset in enumerate(SIDES):
        copy = pltpu.make_async_remote_copy(
            src_ref=stage.at[side],
            dst_ref=landed.at[side ^ 1],
            send_sem=send_sems.at[side],
            recv_sem=recv_sems.at[side ^ 1],
            device_id=peer(offset),
            device_id_type=MESH,
        )
        copy.start()
        copies.append(copy)

    step = 0.5 * SECTION_BETA

    def plane(s):
        return node_fields(
            [x_ref[k, s] for k in range(3)],
            [m_ref[k, s] for k in range(3)],
            [q_ref[k, s] for k in range(5)],
        )

    def moved(fields, axis):
        size = (chord_len, depth)[axis]

        def roll(v):
            return pltpu.roll(v, size - 1, axis=axis)

        return {
            name: [roll(v) for v in value] if isinstance(value, (list, tuple)) else roll(value)
            for name, value in fields.items()
        }

    row_at = lax.broadcasted_iota(jnp.int32, (chord_len, depth), 0)
    lane_at = lax.broadcasted_iota(jnp.int32, (chord_len, depth), 1)

    def inner(s, before):
        here = plane(s)
        ahead = plane(jnp.minimum(s + 1, last))
        span = double_flux(here, ahead)
        span = [jnp.where(s < last, f, 0.0) for f in span]
        chord = double_flux(here, moved(here, 0))
        chord = [jnp.where(row_at < chord_len - 1, f, 0.0) for f in chord]
        normal = double_flux(here, moved(here, 1))
        normal = [jnp.where(lane_at < depth - 1, f, 0.0) for f in normal]
        for k in range(5):
            residual = span[k] - before[k]
            residual = residual + (chord[k] - pltpu.roll(chord[k], 1, axis=0))
            residual = residual + (normal[k] - pltpu.roll(normal[k], 1, axis=1))
            out_ref[k, s] = here["amounts"][k] - step * residual
        return tuple(span)

    zero = jnp.zeros((chord_len, depth), jnp.float32)
    lax.fori_loop(0, length, inner, (zero,) * 5)

    for copy in copies:
        copy.wait()
    span_at, chord_at = lax.axis_index("span"), lax.axis_index("chord")
    spans, chords = lax.axis_size("span"), lax.axis_size("chord")
    edges = (span_at > 0, span_at < spans - 1, chord_at > 0, chord_at < chords - 1)
    for side in range(4):
        row = last * (side % 2)

        def rim(ref, k):
            return ref[k, row] if side < 2 else ref[k, :, row, :]

        here = node_fields(
            [rim(x_ref, k) for k in range(3)],
            [rim(m_ref, k) for k in range(3)],
            [rim(q_ref, k) for k in range(5)],
        )
        there = node_fields(
            [rims_ref[side, k] for k in range(3)],
            [landed[side, k] for k in range(3)],
            [rims_ref[side, 3 + k] for k in range(5)],
        )
        flux = double_flux(there, here) if side % 2 == 0 else double_flux(here, there)
        sign = step if side % 2 == 0 else -step
        for k in range(5):
            add = jnp.where(edges[side], sign * flux[k], 0.0)
            if side < 2:
                out_ref[k, row] = out_ref[k, row] + add
            else:
                out_ref[k, :, row, :] = out_ref[k, :, row, :] + add


def section(node_coords, grid_motion, primitives, rims):
    depth = node_coords.shape[3]
    vmem = pl.BlockSpec(memory_space=pltpu.VMEM)
    return pl.pallas_call(
        flux_kernel,
        out_shape=jax.ShapeDtypeStruct(primitives.shape, jnp.float32),
        in_specs=[vmem] * 4,
        out_specs=vmem,
        scratch_shapes=[
            pltpu.VMEM((4, 3, 16, depth), jnp.float32),
            pltpu.VMEM((4, 3, 16, depth), jnp.float32),
            pltpu.SemaphoreType.DMA((4,)),
            pltpu.SemaphoreType.DMA((4,)),
        ],
        compiler_params=pltpu.CompilerParams(
            collective_id=1, has_side_effects=True, vmem_limit_bytes=32 << 20
        ),
        name="section",
    )(node_coords, grid_motion, primitives, rims)


def body(node_coords, primitives, control_points, coefficients, support_tiles, support_counts):
    coords_t, points, ranges, rims = gather(
        node_coords, primitives, control_points, coefficients, support_tiles, support_counts
    )
    grid_motion = motion(points, ranges, coords_t, node_coords.shape)
    section_state = section(node_coords, grid_motion, primitives, rims)
    return (grid_motion, section_state)


def solution(mesh):
    in_specs = (
        P(None, "span", "chord", None),
        P(None, "span", "chord", None),
        P(None, ("span", "chord"), None),
        P(None, ("span", "chord"), None),
        P("span", "chord", None),
        P("span", "chord"),
    )
    out_specs = (P(None, "span", "chord", None), P(None, "span", "chord", None))
    return jax.shard_map(body, mesh=mesh, in_specs=in_specs, out_specs=out_specs, check_vma=False)
```

```python
import jax
import jax.numpy as jnp
from jax import lax
from jax.experimental import pallas as pl
from jax.experimental.pallas import tpu as pltpu
from jax.sharding import PartitionSpec as P

RADIUS = 12
GAMMA_GAS = 1.4
SECTION_BETA = 0.2
SLOTS = 6
BATCH = 4
FILL = 8
KEPT = 48
NOWHERE = 511 * 64
REACH = 1.001
MESH = pl.DeviceIdType.MESH
AROUND = tuple((a, b) for a in (-1, 0, 1) for b in (-1, 0, 1) if (a, b) != (0, 0))
SIDES = ((-1, 0), (1, 0), (0, -1), (0, 1))


def peer(offset):
    spans, chords = lax.axis_size("span"), lax.axis_size("chord")
    return {
        "span": lax.rem(lax.axis_index("span") + offset[0] + spans, spans),
        "chord": lax.rem(lax.axis_index("chord") + offset[1] + chords, chords),
    }


def meet(offsets):
    barrier = pltpu.get_barrier_semaphore()
    for offset in offsets:
        pl.semaphore_signal(barrier, inc=1, device_id=peer(offset), device_id_type=MESH)
    return lambda: pl.semaphore_wait(barrier, len(offsets))


def gather_kernel(
    x_hbm,
    q_hbm,
    points_hbm,
    coef_hbm,
    tiles_hbm,
    count_ref,
    x_v,
    q_v,
    sorted_ref,
    index_ref,
    first_ref,
    limits_ref,
    rims_ref,
    tile_v,
    own,
    window,
    stage,
    tiles_ref,
    local_sems,
    send_sems,
    recv_sems,
):
    wait_all = meet(AROUND)
    fetches = []
    for src, dst in (
        (points_hbm, tile_v.at[0]),
        (coef_hbm, tile_v.at[1]),
        (tiles_hbm, tiles_ref),
        (x_hbm, x_v),
        (q_hbm, q_v),
    ):
        fetch = pltpu.make_async_copy(src, dst, local_sems.at[len(fetches)])
        fetch.start()
        fetches.append(fetch)
    fetches[0].wait()
    fetches[1].wait()

    scale = 1.0 / RADIUS
    own[...] = jnp.zeros_like(own)
    for half in range(2):
        lanes = pl.ds(64 * half, 64)
        own[0:3, lanes] = tile_v[0, :, 0, :] * scale
        own[3:6, lanes] = tile_v[1, :, 0, :] * 4.0
    wait_all()

    copies = []

    def send(src, dst, offset):
        at = len(copies)
        copy = pltpu.make_async_remote_copy(
            src_ref=src,
            dst_ref=dst,
            send_sem=send_sems.at[at],
            recv_sem=recv_sems.at[at],
            device_id=peer(offset),
            device_id_type=MESH,
        )
        copy.start()
        copies.append(copy)

    for a, b in AROUND:
        send(own, window.at[(1 - a) * 3 + 1 - b], (a, b))
    window[4] = own[...]

    length = x_v.shape[1]
    for fetch in fetches[2:]:
        fetch.wait()
    for side, row in ((2, 0), (3, length - 1)):
        stage[side, 0:3] = x_v[:, :, row, :]
        stage[side, 3:8] = q_v[:, :, row, :]
    for side, row in ((0, 0), (1, length - 1)):
        stage[side, 0:3] = x_v[:, row]
        stage[side, 3:8] = q_v[:, row]
    for side, offset in enumerate(SIDES):
        send(stage.at[side], rims_ref.at[side ^ 1], offset)

    def bounds(block):
        low = jnp.min(jnp.min(block, axis=0), axis=0, keepdims=True) * scale
        high = jnp.max(jnp.max(block, axis=0), axis=0, keepdims=True) * scale
        return low, high

    def interval(block):
        low, high = bounds(block)
        return jnp.min(low, axis=1, keepdims=True), jnp.max(high, axis=1, keepdims=True)

    boxes = (
        [interval(x_v[0, 8 * h : 8 * h + 8]) for h in range(2)],
        [interval(x_v[1, :, 8 * c : 8 * c + 8]) for c in range(2)],
    )
    z_low, z_high = bounds(x_v[2])

    for copy in copies[:8]:
        copy.wait()
    span_at, chord_at = lax.axis_index("span"), lax.axis_index("chord")
    chords = lax.axis_size("chord")
    count = count_ref[0, 0]
    lane = lax.broadcasted_iota(jnp.int32, (8, 128), 1)
    row_at = lax.broadcasted_iota(jnp.int32, (8, 128), 0)

    def picked(slot):
        tile = tiles_ref[0, 0, slot]
        at = (tile // chords - span_at + 1) * 3 + (tile % chords - chord_at + 1)
        return window[jnp.clip(at, 0, 8)]

    groups = SLOTS // 2
    values, keys, keeps, reaches = [], [], [], []
    blank = jnp.zeros((4, 128), jnp.float32)
    for pair in range(groups):
        value = jnp.where(lane < 64, picked(2 * pair), picked(2 * pair + 1))
        used = jnp.where(lane < 64, 2 * pair, 2 * pair + 1) < count
        value = jnp.where((row_at >= 3) & jnp.logical_not(used), 0.0, value)
        values.append(value)
        keys.append(value[2:3])
        apart = []
        for axis in range(2):
            along = value[axis : axis + 1]
            gaps = [jnp.maximum(jnp.maximum(b[0] - along, along - b[1]), 0.0) for b in boxes[axis]]
            apart.append([gap * gap for gap in gaps])
        spare = [REACH * REACH - apart[0][h] - apart[1][c] for h in range(2) for c in range(2)]
        spare = jnp.concatenate(spare + [blank], axis=0)
        near = (spare > 0.0) & used & (row_at < 4)
        keep = jnp.where(near, 1.0, 0.0)
        keeps.append(jnp.concatenate([keep, jnp.zeros_like(keep)], axis=0).astype(jnp.bfloat16))
        reaches.append(jnp.where(near, jnp.sqrt(jnp.maximum(spare, 0.0)) * 1.01 + 0.01, 0.0))

    columns = [jnp.broadcast_to(key, (128, 128)).T for key in keys]
    big_lane = lax.broadcasted_iota(jnp.int32, (128, 128), 1)
    big_row = lax.broadcasted_iota(jnp.int32, (128, 128), 0)

    def flags(mask):
        return jnp.where(mask, 1.0, 0.0).astype(jnp.bfloat16)

    def counted(blocks):
        return sum(
            jnp.dot(keep, block, preferred_element_type=jnp.float32)
            for keep, block in zip(keeps, blocks)
        )

    ahead = []
    for j in range(groups):
        row = []
        for i in range(groups):
            if j < i:
                before = columns[j] <= keys[i]
            elif j > i:
                before = columns[j] < keys[i]
            else:
                before = (columns[j] < keys[i]) | ((columns[j] == keys[i]) & (big_row < big_lane))
            row.append(flags(before))
        ahead.append(jnp.concatenate(row, axis=1))
    rank = counted(ahead)
    first = counted([flags(jnp.concatenate([c, c], axis=1) < z_low - REACH) for c in columns])
    final = counted([flags(jnp.concatenate([c, c], axis=1) <= z_high + REACH) for c in columns])
    for g in range(4):
        first_ref[g] = jnp.broadcast_to(first[g : g + 1], first_ref.shape[1:]).astype(jnp.int32)
    parts = []
    for value, reach in zip(values, reaches):
        one = value.astype(jnp.bfloat16).astype(jnp.float32)
        rest = value - one
        two = rest.astype(jnp.bfloat16).astype(jnp.float32)
        three = rest - two
        parts.append(jnp.concatenate([one, two, three, reach], axis=0).astype(jnp.bfloat16))
    order = big_row.astype(jnp.float32)
    depth = x_v.shape[3]
    step_at = lax.broadcasted_iota(jnp.int32, (KEPT, depth), 0)
    lower = lax.broadcasted_iota(jnp.int32, (KEPT, KEPT), 0) > lax.broadcasted_iota(
        jnp.int32, (KEPT, KEPT), 1
    )
    for g in range(4):
        total = jnp.zeros((32, 128 * groups), jnp.float32)
        for i in range(groups):
            keep = keeps[i][g : g + 1].astype(jnp.float32) > 0.5
            at = jnp.where(keep, rank[g : g + 1, 128 * i : 128 * i + 128], -1.0)
            place = jnp.concatenate([flags(at == order + 128.0 * j) for j in range(groups)], axis=0)
            total = total + lax.dot_general(
                parts[i], place, (((1,), (1,)), ((), ())), preferred_element_type=jnp.float32
            )
        table = total[0:8] + total[8:16] + total[16:24]
        sorted_ref[g, :, 0 : 128 * groups] = table
        sorted_ref[g, :, 128 * groups :] = jnp.zeros((8, 128), jnp.float32)

        index = step_at + first[g : g + 1].astype(jnp.int32)
        bound = final[g : g + 1].astype(jnp.int32)

        def looked(row):
            tiles = [jnp.broadcast_to(row[:, 128 * j : 128 * j + 128], (8, 128)) for j in range(groups)]
            rows = []
            for k in range(KEPT // 8):
                cols = []
                for h in range(depth // 128):
                    want = index[8 * k : 8 * k + 8, 128 * h : 128 * h + 128]
                    found = jnp.zeros((8, 128), jnp.float32)
                    for j, tile in enumerate(tiles):
                        more = jnp.take_along_axis(tile, want & 127, axis=1)
                        found = jnp.where(want >> 7 == j, more, found)
                    cols.append(found)
                rows.append(jnp.concatenate(cols, axis=1))
            return jnp.concatenate(rows, axis=0)

        z = looked(table[2:3])
        reach = looked(total[24 + g : 25 + g])
        inside = (index < bound) & (z > z_low - reach) & (z < z_high + reach)
        skipped = jnp.dot(
            flags(lower), flags(jnp.logical_not(inside)), preferred_element_type=jnp.float32
        )
        code = jnp.where(inside, index * 64 + skipped.astype(jnp.int32), NOWHERE)
        shift = 1
        while shift < KEPT:
            later = pltpu.roll(code, KEPT - shift, axis=0)
            left = jnp.where((code & shift) != 0, NOWHERE, code)
            code = jnp.where(((later & shift) != 0) & (step_at < KEPT - shift), later, left)
            shift = 2 * shift
        index_ref[g] = code >> 6
        number = jnp.sum(jnp.where(inside, 1, 0), axis=0, keepdims=True)
        for h in range(depth // 128):
            cut = slice(128 * h, 128 * h + 128)
            limits = [
                jnp.max(number[:, cut], axis=1, keepdims=True),
                jnp.max((bound - index[0:1])[:, cut], axis=1, keepdims=True),
                jnp.max(bound[:, cut], axis=1, keepdims=True),
            ]
            limits = jnp.where(lane == 0, limits[0], jnp.where(lane == 1, limits[1], limits[2]))
            limits_ref[h, g] = limits
    for copy in copies[8:]:
        copy.wait()


def gather(node_coords, primitives, control_points, coefficients, tiles, counts):
    depth = node_coords.shape[3]
    vmem = pl.BlockSpec(memory_space=pltpu.VMEM)
    hbm = pl.BlockSpec(memory_space=pltpu.HBM)
    f32 = jnp.float32
    return pl.pallas_call(
        gather_kernel,
        out_shape=(
            jax.ShapeDtypeStruct(node_coords.shape, f32),
            jax.ShapeDtypeStruct(primitives.shape, f32),
            jax.ShapeDtypeStruct((4, 8, 64 * SLOTS + 128), f32),
            jax.ShapeDtypeStruct((4, KEPT, depth), jnp.int32),
            jax.ShapeDtypeStruct((4, 8, depth), jnp.int32),
            jax.ShapeDtypeStruct((2, 4, 8, 128), jnp.int32),
            jax.ShapeDtypeStruct((4, 8, 16, depth), f32),
        ),
        in_specs=[hbm] * 5 + [pl.BlockSpec(memory_space=pltpu.SMEM)],
        out_specs=(vmem,) * 7,
        scratch_shapes=[
            pltpu.VMEM((2,) + control_points.shape, f32),
            pltpu.VMEM((8, 128), f32),
            pltpu.VMEM((9, 8, 128), f32),
            pltpu.VMEM((4, 8, 16, depth), f32),
            pltpu.SMEM(tiles.shape, jnp.int32),
            pltpu.SemaphoreType.DMA((5,)),
            pltpu.SemaphoreType.DMA((12,)),
            pltpu.SemaphoreType.DMA((12,)),
        ],
        compiler_params=pltpu.CompilerParams(
            collective_id=0, has_side_effects=True, vmem_limit_bytes=32 << 20
        ),
        name="gather",
    )(
        *(
            pltpu.with_memory_space_constraint(v, pltpu.HBM)
            for v in (node_coords, primitives, control_points, coefficients, tiles)
        ),
        counts,
    )


SPANS_EACH = 4


def motion_kernel(limits_ref, sorted_ref, index_ref, first_ref, x_ref, m_ref, out_hbm, table, sems):
    scale = 1.0 / RADIUS
    size = sorted_ref.shape[2]

    def part(at, carry):
        g, half = at // 2, at % 2
        lanes = pl.ds(pl.multiple_of(half * 128, 128), 128)
        rows = pl.ds(pl.multiple_of(g % 2 * 8, 8), 8)
        number, most, top = (limits_ref[half, g, 0, k] for k in range(3))
        few = most <= KEPT
        number = jnp.where(few, number, most)
        steps = (number + BATCH - 1) // BATCH

        def pick(index, tiles):
            found = jnp.zeros((8, 128), jnp.float32)
            for j in range(tiles):
                more = sorted_ref[g, :, 128 * j : 128 * j + 128]
                more = jnp.take_along_axis(more, index & 127, axis=1)
                found = jnp.where(index >> 7 == j, more, found)
            return found

        def fill(tiles):
            def some(i, carry):
                batch = index_ref[g, pl.ds(pl.multiple_of(i * FILL, 8), FILL), lanes]
                for u in range(FILL):
                    index = jnp.broadcast_to(batch[u : u + 1], (8, 128))
                    table[i * FILL + u] = pick(index, tiles)
                return carry

            lax.fori_loop(0, (number + FILL - 1) // FILL, some, 0)

        @pl.when(few & (top <= 128))
        def _():
            fill(1)

        @pl.when(few & (top > 128))
        def _():
            fill(size // 128 - 1)

        @pl.when(most > KEPT)
        def _():
            first = first_ref[g, :, lanes]

            def some(i, carry):
                for u in range(BATCH):
                    table[i * BATCH + u] = pick(first + (i * BATCH + u), size // 128 - 1)
                return carry

            lax.fori_loop(0, steps, some, 0)

        for piece in range(8 // SPANS_EACH):
            spans = pl.ds(g // 2 * 8 + piece * SPANS_EACH, SPANS_EACH)
            x, y, z = (x_ref[k, spans, rows, lanes] * scale for k in range(3))

            def step(i, total):
                total = list(total)
                for u in range(BATCH):
                    point = [table[i * BATCH + u, v : v + 1, :] for v in range(6)]
                    dx, dy, dz = x - point[0], y - point[1], z - point[2]
                    squared = jnp.maximum(dx * dx + dy * dy + dz * dz, 1e-30)
                    remain = jnp.maximum(1.0 - squared * lax.rsqrt(squared), 0.0)
                    second = remain * remain
                    weight = second * second * (1.25 - remain)
                    for k in range(3):
                        total[k] = total[k] + point[3 + k] * weight
                return tuple(total)

            zero = jnp.zeros_like(x)
            total = lax.fori_loop(0, steps, step, (zero, zero, zero))
            for k in range(3):
                m_ref[k, spans, rows, lanes] = total[k]
        return carry

    for h in range(2):
        lax.fori_loop(4 * h, 4 * h + 4, part, 0)
        spans = pl.ds(8 * h, 8)
        pltpu.make_async_copy(m_ref.at[:, spans], out_hbm.at[:, spans], sems.at[h]).start()
    for h in range(2):
        spans = pl.ds(8 * h, 8)
        pltpu.make_async_copy(m_ref.at[:, spans], out_hbm.at[:, spans], sems.at[h]).wait()


def motion(limits, points, index, first, coords):
    vmem = pl.BlockSpec(memory_space=pltpu.VMEM)
    smem = pl.BlockSpec(memory_space=pltpu.SMEM)
    hbm = pl.BlockSpec(memory_space=pltpu.HBM)
    out = jax.ShapeDtypeStruct(coords.shape, jnp.float32)
    return pl.pallas_call(
        motion_kernel,
        out_shape=(out, out),
        in_specs=[smem, vmem, vmem, vmem, vmem],
        out_specs=(vmem, hbm),
        scratch_shapes=[
            pltpu.VMEM((64 * SLOTS + FILL, 8, 128), jnp.float32),
            pltpu.SemaphoreType.DMA((2,)),
        ],
        compiler_params=pltpu.CompilerParams(vmem_limit_bytes=32 << 20),
        name="motion",
    )(limits, points, index, first, coords)


def node_fields(coords, speed, state):
    rho, u, p = state[0], state[1:4], state[4]
    kinetic = 0.5 * rho * (u[0] * u[0] + u[1] * u[1] + u[2] * u[2])
    return dict(
        place=[a + b for a, b in zip(coords, speed)],
        speed=speed,
        u=u,
        p=p,
        amounts=[rho] + [rho * v for v in u] + [p / (GAMMA_GAS - 1.0) + kinetic],
        sound=jnp.sqrt(GAMMA_GAS * p / rho),
    )


def dot3(a, b):
    return a[0] * b[0] + a[1] * b[1] + a[2] * b[2]


def double_flux(left, right):
    edge = [b - a for a, b in zip(left["place"], right["place"])]
    magnitude = lax.rsqrt(dot3(edge, edge))
    inverse = magnitude * magnitude
    normal = [e * inverse for e in edge]
    frame = 0.5 * dot3([a + b for a, b in zip(left["speed"], right["speed"])], normal)
    left_un, right_un = dot3(left["u"], normal), dot3(right["u"], normal)
    left_rel, right_rel = left_un - frame, right_un - frame
    signal = jnp.maximum(
        jnp.abs(left_rel) + left["sound"] * magnitude,
        jnp.abs(right_rel) + right["sound"] * magnitude,
    )
    left_gain, right_gain = left_rel + signal, right_rel - signal
    flux = [a * left_gain + b * right_gain for a, b in zip(left["amounts"], right["amounts"])]
    pressure = left["p"] + right["p"]
    for k in range(3):
        flux[1 + k] = flux[1 + k] + pressure * normal[k]
    flux[4] = flux[4] + left["p"] * left_un + right["p"] * right_un
    return flux


def flux_kernel(
    x_ref,
    m_ref,
    q_ref,
    rims_ref,
    out_ref,
    stage,
    landed,
    send_sems,
    recv_sems,
):
    wait_all = meet(SIDES)
    length, chord_len, depth = x_ref.shape[1:]
    last = length - 1
    stage[0] = m_ref[:, 0]
    stage[1] = m_ref[:, last]
    stage[2] = m_ref[:, :, 0, :]
    stage[3] = m_ref[:, :, last, :]
    wait_all()
    copies = []
    for side, offset in enumerate(SIDES):
        copy = pltpu.make_async_remote_copy(
            src_ref=stage.at[side],
            dst_ref=landed.at[side ^ 1],
            send_sem=send_sems.at[side],
            recv_sem=recv_sems.at[side ^ 1],
            device_id=peer(offset),
            device_id_type=MESH,
        )
        copy.start()
        copies.append(copy)

    step = 0.5 * SECTION_BETA

    def plane(s):
        return node_fields(
            [x_ref[k, s] for k in range(3)],
            [m_ref[k, s] for k in range(3)],
            [q_ref[k, s] for k in range(5)],
        )

    def moved(fields, axis):
        size = (chord_len, depth)[axis]

        def roll(v):
            return pltpu.roll(v, size - 1, axis=axis)

        return {
            name: [roll(v) for v in value] if isinstance(value, (list, tuple)) else roll(value)
            for name, value in fields.items()
        }

    row_at = lax.broadcasted_iota(jnp.int32, (chord_len, depth), 0)
    lane_at = lax.broadcasted_iota(jnp.int32, (chord_len, depth), 1)

    def inner(s, before):
        here = plane(s)
        ahead = plane(jnp.minimum(s + 1, last))
        span = double_flux(here, ahead)
        span = [jnp.where(s < last, f, 0.0) for f in span]
        chord = double_flux(here, moved(here, 0))
        chord = [jnp.where(row_at < chord_len - 1, f, 0.0) for f in chord]
        normal = double_flux(here, moved(here, 1))
        normal = [jnp.where(lane_at < depth - 1, f, 0.0) for f in normal]
        for k in range(5):
            residual = span[k] - before[k]
            residual = residual + (chord[k] - pltpu.roll(chord[k], 1, axis=0))
            residual = residual + (normal[k] - pltpu.roll(normal[k], 1, axis=1))
            out_ref[k, s] = here["amounts"][k] - step * residual
        return tuple(span)

    zero = jnp.zeros((chord_len, depth), jnp.float32)
    lax.fori_loop(0, length, inner, (zero,) * 5)

    for copy in copies:
        copy.wait()
    span_at, chord_at = lax.axis_index("span"), lax.axis_index("chord")
    spans, chords = lax.axis_size("span"), lax.axis_size("chord")
    edges = (span_at > 0, span_at < spans - 1, chord_at > 0, chord_at < chords - 1)
    for side in range(4):
        row = last * (side % 2)

        def rim(ref, k):
            return ref[k, row] if side < 2 else ref[k, :, row, :]

        here = node_fields(
            [rim(x_ref, k) for k in range(3)],
            [rim(m_ref, k) for k in range(3)],
            [rim(q_ref, k) for k in range(5)],
        )
        there = node_fields(
            [rims_ref[side, k] for k in range(3)],
            [landed[side, k] for k in range(3)],
            [rims_ref[side, 3 + k] for k in range(5)],
        )
        flux = double_flux(there, here) if side % 2 == 0 else double_flux(here, there)
        sign = step if side % 2 == 0 else -step
        for k in range(5):
            add = jnp.where(edges[side], sign * flux[k], 0.0)
            if side < 2:
                out_ref[k, row] = out_ref[k, row] + add
            else:
                out_ref[k, :, row, :] = out_ref[k, :, row, :] + add


def section(node_coords, grid_motion, primitives, rims):
    depth = node_coords.shape[3]
    vmem = pl.BlockSpec(memory_space=pltpu.VMEM)
    return pl.pallas_call(
        flux_kernel,
        out_shape=jax.ShapeDtypeStruct(primitives.shape, jnp.float32),
        in_specs=[vmem] * 4,
        out_specs=vmem,
        scratch_shapes=[
            pltpu.VMEM((4, 3, 16, depth), jnp.float32),
            pltpu.VMEM((4, 3, 16, depth), jnp.float32),
            pltpu.SemaphoreType.DMA((4,)),
            pltpu.SemaphoreType.DMA((4,)),
        ],
        compiler_params=pltpu.CompilerParams(
            collective_id=1, has_side_effects=True, vmem_limit_bytes=32 << 20
        ),
        name="section",
    )(node_coords, grid_motion, primitives, rims)


def body(node_coords, primitives, control_points, coefficients, support_tiles, support_counts):
    coords, states, points, index, first, limits, rims = gather(
        node_coords, primitives, control_points, coefficients, support_tiles, support_counts
    )
    moved, grid_motion = motion(limits, points, index, first, coords)
    section_state = section(coords, moved, states, rims)
    return (grid_motion, section_state)


def solution(mesh):
    in_specs = (
        P(None, "span", "chord", None),
        P(None, "span", "chord", None),
        P(None, ("span", "chord"), None),
        P(None, ("span", "chord"), None),
        P("span", "chord", None),
        P("span", "chord"),
    )
    out_specs = (P(None, "span", "chord", None), P(None, "span", "chord", None))
    return jax.shard_map(body, mesh=mesh, in_specs=in_specs, out_specs=out_specs, check_vma=False)
```

```python
import jax
import jax.numpy as jnp
from jax import lax
from jax.experimental import pallas as pl
from jax.experimental.pallas import tpu as pltpu
from jax.sharding import PartitionSpec as P

RADIUS = 12
GAMMA_GAS = 1.4
SECTION_BETA = 0.2
SLOTS = 6
BATCH = 4
KEPT = 48
EARLY = 16
NOWHERE = 511 * 64
REACH = 1.001
MESH = pl.DeviceIdType.MESH
AROUND = tuple((a, b) for a in (-1, 0, 1) for b in (-1, 0, 1) if (a, b) != (0, 0))
SIDES = ((-1, 0), (1, 0), (0, -1), (0, 1))


def peer(offset):
    spans, chords = lax.axis_size("span"), lax.axis_size("chord")
    return {
        "span": lax.rem(lax.axis_index("span") + offset[0] + spans, spans),
        "chord": lax.rem(lax.axis_index("chord") + offset[1] + chords, chords),
    }


def exists(offset):
    a = lax.axis_index("span") + offset[0]
    b = lax.axis_index("chord") + offset[1]
    return (a >= 0) & (a < lax.axis_size("span")) & (b >= 0) & (b < lax.axis_size("chord"))


def opposite(offset):
    return (-offset[0], -offset[1])


def meet(offsets):
    barrier = pltpu.get_barrier_semaphore()
    for offset in offsets:

        @pl.when(exists(offset))
        def _():
            pl.semaphore_signal(barrier, inc=1, device_id=peer(offset), device_id_type=MESH)

    number = sum(jnp.where(exists(offset), 1, 0) for offset in offsets)
    return lambda: pl.semaphore_wait(barrier, number)


def wait_for(copies):
    for copy, offset in copies:

        @pl.when(exists(offset))
        def _():
            copy.wait_send()

        @pl.when(exists(opposite(offset)))
        def _():
            copy.wait_recv()


def look_up(sorted_ref, g, index, tiles):
    found = jnp.zeros((8, 128), jnp.float32)
    for j in range(tiles):
        more = sorted_ref[g, :, 128 * j : 128 * j + 128]
        more = jnp.take_along_axis(more, index & 127, axis=1)
        found = jnp.where(index >> 7 == j, more, found)
    return found


def add_points(table, steps, nodes, total):
    x, y, z = nodes

    def step(i, total):
        total = list(total)
        for u in range(BATCH):
            point = [table[i * BATCH + u, v : v + 1, :] for v in range(6)]
            dx, dy, dz = x - point[0], y - point[1], z - point[2]
            squared = jnp.maximum(dx * dx + dy * dy + dz * dz, 1e-30)
            remain = jnp.maximum(1.0 - squared * lax.rsqrt(squared), 0.0)
            second = remain * remain
            weight = second * second * (1.25 - remain)
            for k in range(3):
                total[k] = total[k] + point[3 + k] * weight
        return tuple(total)

    return lax.fori_loop(0, steps, step, total)


def part_of(at):
    g, half = at // 2, at % 2
    lanes = pl.ds(pl.multiple_of(half * 128, 128), 128)
    rows = pl.ds(pl.multiple_of(g % 2 * 8, 8), 8)
    pieces = [pl.ds(g // 2 * 8 + k * SPANS_EACH, SPANS_EACH) for k in range(8 // SPANS_EACH)]
    return g, half, lanes, rows, pieces


def gather_kernel(
    x_hbm,
    q_hbm,
    points_hbm,
    coef_hbm,
    tiles_hbm,
    count_ref,
    x_v,
    q_v,
    sorted_ref,
    index_ref,
    first_ref,
    limits_ref,
    part_ref,
    rims_ref,
    tile_v,
    own,
    window,
    stage,
    table,
    tiles_ref,
    local_sems,
    send_sems,
    recv_sems,
):
    window[...] = jnp.zeros_like(window)
    wait_all = meet(AROUND)
    fetches = []
    for src, dst in (
        (points_hbm, tile_v.at[0]),
        (coef_hbm, tile_v.at[1]),
        (tiles_hbm, tiles_ref),
        (x_hbm, x_v),
        (q_hbm, q_v),
    ):
        fetch = pltpu.make_async_copy(src, dst, local_sems.at[len(fetches)])
        fetch.start()
        fetches.append(fetch)
    fetches[0].wait()
    fetches[1].wait()

    scale = 1.0 / RADIUS
    own[...] = jnp.zeros_like(own)
    for half in range(2):
        lanes = pl.ds(64 * half, 64)
        own[0:3, lanes] = tile_v[0, :, 0, :] * scale
        own[3:6, lanes] = tile_v[1, :, 0, :] * 4.0
    wait_all()

    copies = []

    def send(src, dst, offset):
        at = len(copies)
        copy = pltpu.make_async_remote_copy(
            src_ref=src,
            dst_ref=dst,
            send_sem=send_sems.at[at],
            recv_sem=recv_sems.at[at],
            device_id=peer(offset),
            device_id_type=MESH,
        )

        @pl.when(exists(offset))
        def _():
            copy.start()

        copies.append((copy, offset))

    for a, b in AROUND:
        send(own, window.at[(1 - a) * 3 + 1 - b], (a, b))
    window[4] = own[...]

    length = x_v.shape[1]
    for fetch in fetches[2:]:
        fetch.wait()
    for side, row in ((2, 0), (3, length - 1)):
        stage[side, 0:3] = x_v[:, :, row, :]
        stage[side, 3:8] = q_v[:, :, row, :]
    for side, row in ((0, 0), (1, length - 1)):
        stage[side, 0:3] = x_v[:, row]
        stage[side, 3:8] = q_v[:, row]
    for side, offset in enumerate(SIDES):
        send(stage.at[side], rims_ref.at[side ^ 1], offset)

    def bounds(block):
        low = jnp.min(jnp.min(block, axis=0), axis=0, keepdims=True) * scale
        high = jnp.max(jnp.max(block, axis=0), axis=0, keepdims=True) * scale
        return low, high

    def interval(block):
        low, high = bounds(block)
        return jnp.min(low, axis=1, keepdims=True), jnp.max(high, axis=1, keepdims=True)

    boxes = (
        [interval(x_v[0, 8 * h : 8 * h + 8]) for h in range(2)],
        [interval(x_v[1, :, 8 * c : 8 * c + 8]) for c in range(2)],
    )
    z_low, z_high = bounds(x_v[2])

    wait_for(copies[:8])
    span_at, chord_at = lax.axis_index("span"), lax.axis_index("chord")
    chords = lax.axis_size("chord")
    count = count_ref[0, 0]
    lane = lax.broadcasted_iota(jnp.int32, (8, 128), 1)
    row_at = lax.broadcasted_iota(jnp.int32, (8, 128), 0)

    def picked(slot):
        tile = tiles_ref[0, 0, slot]
        at = (tile // chords - span_at + 1) * 3 + (tile % chords - chord_at + 1)
        return window[jnp.where(slot < count, jnp.clip(at, 0, 8), 4)]

    groups = SLOTS // 2
    values, keys, keeps, reaches = [], [], [], []
    blank = jnp.zeros((4, 128), jnp.float32)
    for pair in range(groups):
        value = jnp.where(lane < 64, picked(2 * pair), picked(2 * pair + 1))
        used = jnp.where(lane < 64, 2 * pair, 2 * pair + 1) < count
        value = jnp.where((row_at >= 3) & jnp.logical_not(used), 0.0, value)
        values.append(value)
        keys.append(value[2:3])
        apart = []
        for axis in range(2):
            along = value[axis : axis + 1]
            gaps = [jnp.maximum(jnp.maximum(b[0] - along, along - b[1]), 0.0) for b in boxes[axis]]
            apart.append([gap * gap for gap in gaps])
        spare = [REACH * REACH - apart[0][h] - apart[1][c] for h in range(2) for c in range(2)]
        spare = jnp.concatenate(spare + [blank], axis=0)
        near = (spare > 0.0) & used & (row_at < 4)
        keep = jnp.where(near, 1.0, 0.0)
        keeps.append(jnp.concatenate([keep, jnp.zeros_like(keep)], axis=0).astype(jnp.bfloat16))
        reaches.append(jnp.where(near, jnp.sqrt(jnp.maximum(spare, 0.0)) * 1.01 + 0.01, 0.0))

    columns = [jnp.broadcast_to(key, (128, 128)).T for key in keys]
    big_lane = lax.broadcasted_iota(jnp.int32, (128, 128), 1)
    big_row = lax.broadcasted_iota(jnp.int32, (128, 128), 0)

    def flags(mask):
        return jnp.where(mask, 1.0, 0.0).astype(jnp.bfloat16)

    def counted(blocks):
        return sum(
            jnp.dot(keep, block, preferred_element_type=jnp.float32)
            for keep, block in zip(keeps, blocks)
        )

    ahead = []
    for j in range(groups):
        row = []
        for i in range(groups):
            if j < i:
                before = columns[j] <= keys[i]
            elif j > i:
                before = columns[j] < keys[i]
            else:
                before = (columns[j] < keys[i]) | ((columns[j] == keys[i]) & (big_row < big_lane))
            row.append(flags(before))
        ahead.append(jnp.concatenate(row, axis=1))
    rank = counted(ahead)
    first = counted([flags(jnp.concatenate([c, c], axis=1) < z_low - REACH) for c in columns])
    final = counted([flags(jnp.concatenate([c, c], axis=1) <= z_high + REACH) for c in columns])
    for g in range(4):
        first_ref[g] = jnp.broadcast_to(first[g : g + 1], first_ref.shape[1:]).astype(jnp.int32)
    parts = []
    for value, reach in zip(values, reaches):
        one = value.astype(jnp.bfloat16).astype(jnp.float32)
        rest = value - one
        two = rest.astype(jnp.bfloat16).astype(jnp.float32)
        three = rest - two
        parts.append(jnp.concatenate([one, two, three, reach], axis=0).astype(jnp.bfloat16))
    order = big_row.astype(jnp.float32)
    depth = x_v.shape[3]
    step_at = lax.broadcasted_iota(jnp.int32, (KEPT, depth), 0)
    lower = lax.broadcasted_iota(jnp.int32, (KEPT, KEPT), 0) > lax.broadcasted_iota(
        jnp.int32, (KEPT, KEPT), 1
    )
    for g in range(4):
        total = jnp.zeros((32, 128 * groups), jnp.float32)
        for i in range(groups):
            keep = keeps[i][g : g + 1].astype(jnp.float32) > 0.5
            at = jnp.where(keep, rank[g : g + 1, 128 * i : 128 * i + 128], -1.0)
            place = jnp.concatenate([flags(at == order + 128.0 * j) for j in range(groups)], axis=0)
            total = total + lax.dot_general(
                parts[i], place, (((1,), (1,)), ((), ())), preferred_element_type=jnp.float32
            )
        listed = total[0:8] + total[8:16] + total[16:24]
        sorted_ref[g, :, 0 : 128 * groups] = listed
        sorted_ref[g, :, 128 * groups :] = jnp.zeros((8, 128), jnp.float32)

        index = step_at + first[g : g + 1].astype(jnp.int32)
        bound = final[g : g + 1].astype(jnp.int32)

        def looked(row):
            tiles = [jnp.broadcast_to(row[:, 128 * j : 128 * j + 128], (8, 128)) for j in range(groups)]
            rows = []
            for k in range(KEPT // 8):
                cols = []
                for h in range(depth // 128):
                    want = index[8 * k : 8 * k + 8, 128 * h : 128 * h + 128]
                    found = jnp.zeros((8, 128), jnp.float32)
                    for j, tile in enumerate(tiles):
                        more = jnp.take_along_axis(tile, want & 127, axis=1)
                        found = jnp.where(want >> 7 == j, more, found)
                    cols.append(found)
                rows.append(jnp.concatenate(cols, axis=1))
            return jnp.concatenate(rows, axis=0)

        z = looked(listed[2:3])
        reach = looked(total[24 + g : 25 + g])
        inside = (index < bound) & (z > z_low - reach) & (z < z_high + reach)
        skipped = jnp.dot(
            flags(lower), flags(jnp.logical_not(inside)), preferred_element_type=jnp.float32
        )
        code = jnp.where(inside, index * 64 + skipped.astype(jnp.int32), NOWHERE)
        shift = 1
        while shift < KEPT:
            later = pltpu.roll(code, KEPT - shift, axis=0)
            left = jnp.where((code & shift) != 0, NOWHERE, code)
            code = jnp.where(((later & shift) != 0) & (step_at < KEPT - shift), later, left)
            shift = 2 * shift
        index_ref[g] = code >> 6
        number = jnp.sum(jnp.where(inside, 1, 0), axis=0, keepdims=True)
        for h in range(depth // 128):
            cut = slice(128 * h, 128 * h + 128)
            limits = [
                jnp.max(number[:, cut], axis=1, keepdims=True),
                jnp.max((bound - index[0:1])[:, cut], axis=1, keepdims=True),
                jnp.max(bound[:, cut], axis=1, keepdims=True),
            ]
            limits = jnp.where(lane == 0, limits[0], jnp.where(lane == 1, limits[1], limits[2]))
            limits_ref[h, g] = limits
    def early(at, carry):
        g, half, lanes, rows, pieces = part_of(at)
        for i in range(EARLY // 8):
            batch = index_ref[g, 8 * i : 8 * i + 8, lanes]
            for u in range(8):
                index = jnp.broadcast_to(batch[u : u + 1], (8, 128))
                table[8 * i + u] = look_up(sorted_ref, g, index, groups)
        for spans in pieces:
            nodes = [x_v[k, spans, rows, lanes] * scale for k in range(3)]
            zero = jnp.zeros_like(nodes[0])
            total = add_points(table, EARLY // BATCH, nodes, (zero, zero, zero))
            for k in range(3):
                part_ref[k, spans, rows, lanes] = total[k]
        return carry

    lax.fori_loop(0, 8, early, 0)
    wait_for(copies[8:])


def gather(node_coords, primitives, control_points, coefficients, tiles, counts):
    depth = node_coords.shape[3]
    vmem = pl.BlockSpec(memory_space=pltpu.VMEM)
    hbm = pl.BlockSpec(memory_space=pltpu.HBM)
    f32 = jnp.float32
    return pl.pallas_call(
        gather_kernel,
        out_shape=(
            jax.ShapeDtypeStruct(node_coords.shape, f32),
            jax.ShapeDtypeStruct(primitives.shape, f32),
            jax.ShapeDtypeStruct((4, 8, 64 * SLOTS + 128), f32),
            jax.ShapeDtypeStruct((4, KEPT, depth), jnp.int32),
            jax.ShapeDtypeStruct((4, 8, depth), jnp.int32),
            jax.ShapeDtypeStruct((2, 4, 8, 128), jnp.int32),
            jax.ShapeDtypeStruct(node_coords.shape, f32),
            jax.ShapeDtypeStruct((4, 8, 16, depth), f32),
        ),
        in_specs=[hbm] * 5 + [pl.BlockSpec(memory_space=pltpu.SMEM)],
        out_specs=(vmem,) * 8,
        scratch_shapes=[
            pltpu.VMEM((2,) + control_points.shape, f32),
            pltpu.VMEM((8, 128), f32),
            pltpu.VMEM((9, 8, 128), f32),
            pltpu.VMEM((4, 8, 16, depth), f32),
            pltpu.VMEM((EARLY, 8, 128), f32),
            pltpu.SMEM(tiles.shape, jnp.int32),
            pltpu.SemaphoreType.DMA((5,)),
            pltpu.SemaphoreType.DMA((12,)),
            pltpu.SemaphoreType.DMA((12,)),
        ],
        compiler_params=pltpu.CompilerParams(
            collective_id=0, has_side_effects=True, vmem_limit_bytes=32 << 20
        ),
        name="gather",
    )(
        *(
            pltpu.with_memory_space_constraint(v, pltpu.HBM)
            for v in (node_coords, primitives, control_points, coefficients, tiles)
        ),
        counts,
    )


SPANS_EACH = 4


def motion_kernel(
    limits_ref, sorted_ref, index_ref, first_ref, x_ref, part_ref, m_ref, out_hbm, table, sems
):
    scale = 1.0 / RADIUS
    tiles = sorted_ref.shape[2] // 128 - 1

    def part(at, carry):
        g, half, lanes, rows, pieces = part_of(at)
        number, most, top = (limits_ref[half, g, 0, k] for k in range(3))
        few = most <= KEPT
        number = jnp.where(few, jnp.maximum(number - EARLY, 0), most)

        def fill(tiles):
            def some(i, carry):
                start = pl.multiple_of(EARLY + i * 8, 8)
                batch = index_ref[g, pl.ds(start, 8), lanes]
                for u in range(8):
                    index = jnp.broadcast_to(batch[u : u + 1], (8, 128))
                    table[i * 8 + u] = look_up(sorted_ref, g, index, tiles)
                return carry

            lax.fori_loop(0, (number + 7) // 8, some, 0)

        @pl.when(few & (top <= 128))
        def _():
            fill(1)

        @pl.when(few & (top > 128))
        def _():
            fill(tiles)

        @pl.when(most > KEPT)
        def _():
            first = first_ref[g, :, lanes]

            def some(i, carry):
                for u in range(BATCH):
                    at = i * BATCH + u
                    table[at] = look_up(sorted_ref, g, first + at, tiles)
                return carry

            lax.fori_loop(0, (number + BATCH - 1) // BATCH, some, 0)

        for spans in pieces:
            nodes = [x_ref[k, spans, rows, lanes] * scale for k in range(3)]
            total = tuple(jnp.where(few, part_ref[k, spans, rows, lanes], 0.0) for k in range(3))
            total = add_points(table, (number + BATCH - 1) // BATCH, nodes, total)
            for k in range(3):
                m_ref[k, spans, rows, lanes] = total[k]
        return carry

    for h in range(2):
        lax.fori_loop(4 * h, 4 * h + 4, part, 0)
        spans = pl.ds(8 * h, 8)
        pltpu.make_async_copy(m_ref.at[:, spans], out_hbm.at[:, spans], sems.at[h]).start()
    for h in range(2):
        spans = pl.ds(8 * h, 8)
        pltpu.make_async_copy(m_ref.at[:, spans], out_hbm.at[:, spans], sems.at[h]).wait()


def motion(limits, points, index, first, coords, begun):
    vmem = pl.BlockSpec(memory_space=pltpu.VMEM)
    smem = pl.BlockSpec(memory_space=pltpu.SMEM)
    hbm = pl.BlockSpec(memory_space=pltpu.HBM)
    out = jax.ShapeDtypeStruct(coords.shape, jnp.float32)
    return pl.pallas_call(
        motion_kernel,
        out_shape=(out, out),
        in_specs=[smem, vmem, vmem, vmem, vmem, vmem],
        out_specs=(vmem, hbm),
        scratch_shapes=[
            pltpu.VMEM((64 * SLOTS + 8, 8, 128), jnp.float32),
            pltpu.SemaphoreType.DMA((2,)),
        ],
        compiler_params=pltpu.CompilerParams(vmem_limit_bytes=32 << 20),
        name="motion",
    )(limits, points, index, first, coords, begun)


def node_fields(coords, speed, state):
    rho, u, p = state[0], state[1:4], state[4]
    kinetic = 0.5 * rho * (u[0] * u[0] + u[1] * u[1] + u[2] * u[2])
    return dict(
        place=[a + b for a, b in zip(coords, speed)],
        speed=speed,
        u=u,
        p=p,
        amounts=[rho] + [rho * v for v in u] + [p / (GAMMA_GAS - 1.0) + kinetic],
        sound=jnp.sqrt(GAMMA_GAS * p / rho),
    )


def dot3(a, b):
    return a[0] * b[0] + a[1] * b[1] + a[2] * b[2]


def double_flux(left, right):
    edge = [b - a for a, b in zip(left["place"], right["place"])]
    magnitude = lax.rsqrt(dot3(edge, edge))
    inverse = magnitude * magnitude
    normal = [e * inverse for e in edge]
    frame = 0.5 * dot3([a + b for a, b in zip(left["speed"], right["speed"])], normal)
    left_un, right_un = dot3(left["u"], normal), dot3(right["u"], normal)
    left_rel, right_rel = left_un - frame, right_un - frame
    signal = jnp.maximum(
        jnp.abs(left_rel) + left["sound"] * magnitude,
        jnp.abs(right_rel) + right["sound"] * magnitude,
    )
    left_gain, right_gain = left_rel + signal, right_rel - signal
    flux = [a * left_gain + b * right_gain for a, b in zip(left["amounts"], right["amounts"])]
    pressure = left["p"] + right["p"]
    for k in range(3):
        flux[1 + k] = flux[1 + k] + pressure * normal[k]
    flux[4] = flux[4] + left["p"] * left_un + right["p"] * right_un
    return flux


def flux_kernel(
    x_ref,
    m_ref,
    q_ref,
    rims_ref,
    out_ref,
    stage,
    landed,
    send_sems,
    recv_sems,
):
    wait_all = meet(SIDES)
    length, chord_len, depth = x_ref.shape[1:]
    last = length - 1
    stage[0] = m_ref[:, 0]
    stage[1] = m_ref[:, last]
    stage[2] = m_ref[:, :, 0, :]
    stage[3] = m_ref[:, :, last, :]
    copies = []
    for side, offset in enumerate(SIDES):
        copy = pltpu.make_async_remote_copy(
            src_ref=stage.at[side],
            dst_ref=landed.at[side ^ 1],
            send_sem=send_sems.at[side],
            recv_sem=recv_sems.at[side ^ 1],
            device_id=peer(offset),
            device_id_type=MESH,
        )
        copies.append((copy, offset))

    step = 0.5 * SECTION_BETA

    def plane(s):
        return node_fields(
            [x_ref[k, s] for k in range(3)],
            [m_ref[k, s] for k in range(3)],
            [q_ref[k, s] for k in range(5)],
        )

    def moved(fields, axis):
        size = (chord_len, depth)[axis]

        def roll(v):
            return pltpu.roll(v, size - 1, axis=axis)

        return {
            name: [roll(v) for v in value] if isinstance(value, (list, tuple)) else roll(value)
            for name, value in fields.items()
        }

    row_at = lax.broadcasted_iota(jnp.int32, (chord_len, depth), 0)
    lane_at = lax.broadcasted_iota(jnp.int32, (chord_len, depth), 1)

    def inner(s, before):
        here = plane(s)
        ahead = plane(jnp.minimum(s + 1, last))
        span = double_flux(here, ahead)
        span = [jnp.where(s < last, f, 0.0) for f in span]
        chord = double_flux(here, moved(here, 0))
        chord = [jnp.where(row_at < chord_len - 1, f, 0.0) for f in chord]
        normal = double_flux(here, moved(here, 1))
        normal = [jnp.where(lane_at < depth - 1, f, 0.0) for f in normal]
        for k in range(5):
            residual = span[k] - before[k]
            residual = residual + (chord[k] - pltpu.roll(chord[k], 1, axis=0))
            residual = residual + (normal[k] - pltpu.roll(normal[k], 1, axis=1))
            out_ref[k, s] = here["amounts"][k] - step * residual
        return tuple(span)

    zero = jnp.zeros((chord_len, depth), jnp.float32)
    before = lax.fori_loop(0, length // 2, inner, (zero,) * 5)
    wait_all()
    for copy, offset in copies:

        @pl.when(exists(offset))
        def _():
            copy.start()

    lax.fori_loop(length // 2, length, inner, before)
    wait_for(copies)
    def add_rim(side):
        row = last * (side % 2)

        def rim(ref, k):
            return ref[k, row] if side < 2 else ref[k, :, row, :]

        here = node_fields(
            [rim(x_ref, k) for k in range(3)],
            [rim(m_ref, k) for k in range(3)],
            [rim(q_ref, k) for k in range(5)],
        )
        there = node_fields(
            [rims_ref[side, k] for k in range(3)],
            [landed[side, k] for k in range(3)],
            [rims_ref[side, 3 + k] for k in range(5)],
        )
        flux = double_flux(there, here) if side % 2 == 0 else double_flux(here, there)
        sign = step if side % 2 == 0 else -step
        for k in range(5):
            add = sign * flux[k]
            if side < 2:
                out_ref[k, row] = out_ref[k, row] + add
            else:
                out_ref[k, :, row, :] = out_ref[k, :, row, :] + add

    for side, offset in enumerate(SIDES):
        pl.when(exists(offset))(lambda: add_rim(side))


def section(node_coords, grid_motion, primitives, rims):
    depth = node_coords.shape[3]
    vmem = pl.BlockSpec(memory_space=pltpu.VMEM)
    return pl.pallas_call(
        flux_kernel,
        out_shape=jax.ShapeDtypeStruct(primitives.shape, jnp.float32),
        in_specs=[vmem] * 4,
        out_specs=vmem,
        scratch_shapes=[
            pltpu.VMEM((4, 3, 16, depth), jnp.float32),
            pltpu.VMEM((4, 3, 16, depth), jnp.float32),
            pltpu.SemaphoreType.DMA((4,)),
            pltpu.SemaphoreType.DMA((4,)),
        ],
        compiler_params=pltpu.CompilerParams(
            collective_id=1, has_side_effects=True, vmem_limit_bytes=32 << 20
        ),
        name="section",
    )(node_coords, grid_motion, primitives, rims)


def body(node_coords, primitives, control_points, coefficients, support_tiles, support_counts):
    coords, states, points, index, first, limits, begun, rims = gather(
        node_coords, primitives, control_points, coefficients, support_tiles, support_counts
    )
    moved, grid_motion = motion(limits, points, index, first, coords, begun)
    section_state = section(coords, moved, states, rims)
    return (grid_motion, section_state)


def solution(mesh):
    in_specs = (
        P(None, "span", "chord", None),
        P(None, "span", "chord", None),
        P(None, ("span", "chord"), None),
        P(None, ("span", "chord"), None),
        P("span", "chord", None),
        P("span", "chord"),
    )
    out_specs = (P(None, "span", "chord", None), P(None, "span", "chord", None))
    return jax.shard_map(body, mesh=mesh, in_specs=in_specs, out_specs=out_specs, check_vma=False)
```

```python
import jax
import jax.numpy as jnp
from jax import lax
from jax.experimental import pallas as pl
from jax.experimental.pallas import tpu as pltpu
from jax.sharding import PartitionSpec as P

RADIUS = 12
GAMMA_GAS = 1.4
SECTION_BETA = 0.2
SLOTS = 6
BATCH = 4
KEPT = 48
EARLY = 16
AHEAD = 4
NOWHERE = 511 * 64
REACH = 1.001
MESH = pl.DeviceIdType.MESH
AROUND = tuple((a, b) for a in (-1, 0, 1) for b in (-1, 0, 1) if (a, b) != (0, 0))
SIDES = ((-1, 0), (1, 0), (0, -1), (0, 1))


def peer(offset):
    spans, chords = lax.axis_size("span"), lax.axis_size("chord")
    return {
        "span": lax.rem(lax.axis_index("span") + offset[0] + spans, spans),
        "chord": lax.rem(lax.axis_index("chord") + offset[1] + chords, chords),
    }


def exists(offset):
    a = lax.axis_index("span") + offset[0]
    b = lax.axis_index("chord") + offset[1]
    return (a >= 0) & (a < lax.axis_size("span")) & (b >= 0) & (b < lax.axis_size("chord"))


def opposite(offset):
    return (-offset[0], -offset[1])


def meet(offsets):
    barrier = pltpu.get_barrier_semaphore()
    for offset in offsets:

        @pl.when(exists(offset))
        def _():
            pl.semaphore_signal(barrier, inc=1, device_id=peer(offset), device_id_type=MESH)

    number = sum(jnp.where(exists(offset), 1, 0) for offset in offsets)
    return lambda: pl.semaphore_wait(barrier, number)


def wait_for(copies):
    for copy, offset in copies:

        @pl.when(exists(offset))
        def _():
            copy.wait_send()

        @pl.when(exists(opposite(offset)))
        def _():
            copy.wait_recv()


def look_up(sorted_ref, g, index, tiles):
    found = jnp.zeros((8, 128), jnp.float32)
    for j in range(tiles):
        more = sorted_ref[g, :, 128 * j : 128 * j + 128]
        more = jnp.take_along_axis(more, index & 127, axis=1)
        found = jnp.where(index >> 7 == j, more, found)
    return found


def add_points(table, steps, nodes, total):
    x, y, z = nodes

    def step(i, total):
        total = list(total)
        for u in range(BATCH):
            point = [table[i * BATCH + u, v : v + 1, :] for v in range(6)]
            dx, dy, dz = x - point[0], y - point[1], z - point[2]
            squared = jnp.maximum(dx * dx + dy * dy + dz * dz, 1e-30)
            remain = jnp.maximum(1.0 - squared * lax.rsqrt(squared), 0.0)
            second = remain * remain
            weight = second * second * (1.25 - remain)
            for k in range(3):
                total[k] = total[k] + point[3 + k] * weight
        return tuple(total)

    return lax.fori_loop(0, steps, step, total)


def part_of(at):
    g, half = at // 2, at % 2
    lanes = pl.ds(pl.multiple_of(half * 128, 128), 128)
    rows = pl.ds(pl.multiple_of(g % 2 * 8, 8), 8)
    pieces = [pl.ds(g // 2 * 8 + k * SPANS_EACH, SPANS_EACH) for k in range(8 // SPANS_EACH)]
    return g, half, lanes, rows, pieces


def start_far_first(copies):
    core = lax.rem(lax.axis_index("chord"), 2)
    for side, wanted in ((2, core == 0), (3, core == 1), (0, True), (1, True), (3, core == 0), (2, core == 1)):
        copy, offset = copies[side]

        @pl.when(exists(offset) & wanted)
        def _():
            copy.start()


def add_first(sorted_ref, index_ref, table, x_ref, out_ref):
    tiles = sorted_ref.shape[2] // 128 - 1

    def part(at, carry):
        g, half, lanes, rows, pieces = part_of(at)
        for i in range(0, EARLY, 8):
            batch = index_ref[g, i : i + 8, lanes]
            for u in range(8):
                index = jnp.broadcast_to(batch[u : u + 1], (8, 128))
                table[i + u] = look_up(sorted_ref, g, index, tiles)
        for spans in pieces:
            nodes = [x_ref[k, spans, rows, lanes] * (1.0 / RADIUS) for k in range(3)]
            total = add_points(table, EARLY // BATCH, nodes, (jnp.zeros_like(nodes[0]),) * 3)
            for k in range(3):
                out_ref[k, spans, rows, lanes] = total[k]
        return carry

    lax.fori_loop(0, 8, part, 0)


def gather_kernel(
    x_hbm,
    q_hbm,
    points_hbm,
    coef_hbm,
    tiles_hbm,
    count_ref,
    x_v,
    q_v,
    sorted_ref,
    index_ref,
    first_ref,
    limits_ref,
    part_ref,
    rims_ref,
    tile_v,
    own,
    window,
    stage,
    table,
    tiles_ref,
    local_sems,
    send_sems,
    recv_sems,
):
    window[...] = jnp.zeros_like(window)
    wait_all = meet(AROUND)
    fetches = []
    for src, dst in (
        (points_hbm, tile_v.at[0]),
        (coef_hbm, tile_v.at[1]),
        (tiles_hbm, tiles_ref),
        (x_hbm, x_v),
        (q_hbm, q_v),
    ):
        fetch = pltpu.make_async_copy(src, dst, local_sems.at[len(fetches)])
        fetch.start()
        fetches.append(fetch)
    fetches[0].wait()
    fetches[1].wait()

    scale = 1.0 / RADIUS
    own[...] = jnp.zeros_like(own)
    for half in range(2):
        lanes = pl.ds(64 * half, 64)
        own[0:3, lanes] = tile_v[0, :, 0, :] * scale
        own[3:6, lanes] = tile_v[1, :, 0, :] * 4.0
    wait_all()

    copies = []

    def remote(src, dst, offset):
        at = len(copies)
        copy = pltpu.make_async_remote_copy(
            src_ref=src,
            dst_ref=dst,
            send_sem=send_sems.at[at],
            recv_sem=recv_sems.at[at],
            device_id=peer(offset),
            device_id_type=MESH,
        )
        copies.append((copy, offset))

    for a, b in AROUND:
        remote(own, window.at[(1 - a) * 3 + 1 - b], (a, b))
        pl.when(exists((a, b)))(copies[-1][0].start)
    window[4] = own[...]

    length = x_v.shape[1]
    for fetch in fetches[2:]:
        fetch.wait()
    for side, row in ((2, 0), (3, length - 1)):
        stage[side, 0:3] = x_v[:, :, row, :]
        stage[side, 3:8] = q_v[:, :, row, :]
    for side, row in ((0, 0), (1, length - 1)):
        stage[side, 0:3] = x_v[:, row]
        stage[side, 3:8] = q_v[:, row]
    for side, offset in enumerate(SIDES):
        remote(stage.at[side], rims_ref.at[side ^ 1], offset)
    start_far_first(copies[8:])

    def bounds(block):
        low = jnp.min(jnp.min(block, axis=0), axis=0, keepdims=True) * scale
        high = jnp.max(jnp.max(block, axis=0), axis=0, keepdims=True) * scale
        return low, high

    def interval(block):
        low, high = bounds(block)
        return jnp.min(low, axis=1, keepdims=True), jnp.max(high, axis=1, keepdims=True)

    boxes = (
        [interval(x_v[0, 8 * h : 8 * h + 8]) for h in range(2)],
        [interval(x_v[1, :, 8 * c : 8 * c + 8]) for c in range(2)],
    )
    z_low, z_high = bounds(x_v[2])

    wait_for(copies[:8])
    span_at, chord_at = lax.axis_index("span"), lax.axis_index("chord")
    chords = lax.axis_size("chord")
    count = count_ref[0, 0]
    lane = lax.broadcasted_iota(jnp.int32, (8, 128), 1)
    row_at = lax.broadcasted_iota(jnp.int32, (8, 128), 0)

    def picked(slot):
        tile = tiles_ref[0, 0, slot]
        at = (tile // chords - span_at + 1) * 3 + (tile % chords - chord_at + 1)
        return window[jnp.where(slot < count, jnp.clip(at, 0, 8), 4)]

    groups = SLOTS // 2
    values, keys, keeps, reaches = [], [], [], []
    blank = jnp.zeros((4, 128), jnp.float32)
    for pair in range(groups):
        value = jnp.where(lane < 64, picked(2 * pair), picked(2 * pair + 1))
        used = jnp.where(lane < 64, 2 * pair, 2 * pair + 1) < count
        value = jnp.where((row_at >= 3) & jnp.logical_not(used), 0.0, value)
        values.append(value)
        keys.append(value[2:3])
        apart = []
        for axis in range(2):
            along = value[axis : axis + 1]
            gaps = [jnp.maximum(jnp.maximum(b[0] - along, along - b[1]), 0.0) for b in boxes[axis]]
            apart.append([gap * gap for gap in gaps])
        spare = [REACH * REACH - apart[0][h] - apart[1][c] for h in range(2) for c in range(2)]
        spare = jnp.concatenate(spare + [blank], axis=0)
        near = (spare > 0.0) & used & (row_at < 4)
        keep = jnp.where(near, 1.0, 0.0)
        keeps.append(jnp.concatenate([keep, jnp.zeros_like(keep)], axis=0).astype(jnp.bfloat16))
        reaches.append(jnp.where(near, jnp.sqrt(jnp.maximum(spare, 0.0)) * 1.01 + 0.01, 0.0))

    columns = [jnp.broadcast_to(key, (128, 128)).T for key in keys]
    big_lane = lax.broadcasted_iota(jnp.int32, (128, 128), 1)
    big_row = lax.broadcasted_iota(jnp.int32, (128, 128), 0)

    def flags(mask):
        return jnp.where(mask, 1.0, 0.0).astype(jnp.bfloat16)

    def counted(blocks):
        return sum(
            jnp.dot(keep, block, preferred_element_type=jnp.float32)
            for keep, block in zip(keeps, blocks)
        )

    ahead = []
    for j in range(groups):
        row = []
        for i in range(groups):
            if j < i:
                before = columns[j] <= keys[i]
            elif j > i:
                before = columns[j] < keys[i]
            else:
                before = (columns[j] < keys[i]) | ((columns[j] == keys[i]) & (big_row < big_lane))
            row.append(flags(before))
        ahead.append(jnp.concatenate(row, axis=1))
    rank = counted(ahead)
    first = counted([flags(jnp.concatenate([c, c], axis=1) < z_low - REACH) for c in columns])
    final = counted([flags(jnp.concatenate([c, c], axis=1) <= z_high + REACH) for c in columns])
    for g in range(4):
        first_ref[g] = jnp.broadcast_to(first[g : g + 1], first_ref.shape[1:]).astype(jnp.int32)
    parts = []
    for value, reach in zip(values, reaches):
        one = value.astype(jnp.bfloat16).astype(jnp.float32)
        rest = value - one
        two = rest.astype(jnp.bfloat16).astype(jnp.float32)
        three = rest - two
        parts.append(jnp.concatenate([one, two, three, reach], axis=0).astype(jnp.bfloat16))
    order = big_row.astype(jnp.float32)
    depth = x_v.shape[3]
    step_at = lax.broadcasted_iota(jnp.int32, (KEPT, depth), 0)
    lower = lax.broadcasted_iota(jnp.int32, (KEPT, KEPT), 0) > lax.broadcasted_iota(
        jnp.int32, (KEPT, KEPT), 1
    )
    limits = jnp.zeros((8, 128), jnp.int32)
    for g in range(4):
        total = jnp.zeros((32, 128 * groups), jnp.float32)
        for i in range(groups):
            keep = keeps[i][g : g + 1].astype(jnp.float32) > 0.5
            at = jnp.where(keep, rank[g : g + 1, 128 * i : 128 * i + 128], -1.0)
            place = jnp.concatenate([flags(at == order + 128.0 * j) for j in range(groups)], axis=0)
            total = total + lax.dot_general(
                parts[i], place, (((1,), (1,)), ((), ())), preferred_element_type=jnp.float32
            )
        listed = total[0:8] + total[8:16] + total[16:24]
        sorted_ref[g, :, 0 : 128 * groups] = listed
        sorted_ref[g, :, 128 * groups :] = jnp.zeros((8, 128), jnp.float32)

        index = step_at + first[g : g + 1].astype(jnp.int32)
        bound = final[g : g + 1].astype(jnp.int32)

        def looked(row):
            tiles = [jnp.broadcast_to(row[:, 128 * j : 128 * j + 128], (8, 128)) for j in range(groups)]
            rows = []
            for k in range(KEPT // 8):
                cols = []
                for h in range(depth // 128):
                    want = index[8 * k : 8 * k + 8, 128 * h : 128 * h + 128]
                    found = jnp.zeros((8, 128), jnp.float32)
                    for j, tile in enumerate(tiles):
                        more = jnp.take_along_axis(tile, want & 127, axis=1)
                        found = jnp.where(want >> 7 == j, more, found)
                    cols.append(found)
                rows.append(jnp.concatenate(cols, axis=1))
            return jnp.concatenate(rows, axis=0)

        z = looked(listed[2:3])
        reach = looked(total[24 + g : 25 + g])
        inside = (index < bound) & (z > z_low - reach) & (z < z_high + reach)
        skipped = jnp.dot(
            flags(lower), flags(jnp.logical_not(inside)), preferred_element_type=jnp.float32
        )
        code = jnp.where(inside, index * 64 + skipped.astype(jnp.int32), NOWHERE)
        shift = 1
        while shift < KEPT:
            later = pltpu.roll(code, KEPT - shift, axis=0)
            left = jnp.where((code & shift) != 0, NOWHERE, code)
            code = jnp.where(((later & shift) != 0) & (step_at < KEPT - shift), later, left)
            shift = 2 * shift
        number = jnp.sum(jnp.where(inside, 1, 0), axis=0, keepdims=True)
        for h in range(depth // 128):
            cut = slice(128 * h, 128 * h + 128)
            most = jnp.max((bound - index[0:1])[:, cut], axis=1, keepdims=True)
            places = jnp.where(most <= KEPT, code[:, cut] >> 6, NOWHERE >> 6)
            index_ref[g, :, cut] = places
            found = (
                jnp.max(number[:, cut], axis=1, keepdims=True),
                most,
                jnp.max(bound[:, cut], axis=1, keepdims=True),
            )
            for i, limit in enumerate(found):
                limits = jnp.where((row_at == g) & (lane == 3 * h + i), limit, limits)
    limits_ref[...] = limits
    add_first(sorted_ref, index_ref, table, x_v, part_ref)
    wait_for(copies[8:])


def gather(node_coords, primitives, control_points, coefficients, tiles, counts):
    depth = node_coords.shape[3]
    vmem = pl.BlockSpec(memory_space=pltpu.VMEM)
    hbm = pl.BlockSpec(memory_space=pltpu.HBM)
    f32 = jnp.float32
    return pl.pallas_call(
        gather_kernel,
        out_shape=(
            jax.ShapeDtypeStruct(node_coords.shape, f32),
            jax.ShapeDtypeStruct(primitives.shape, f32),
            jax.ShapeDtypeStruct((4, 8, 64 * SLOTS + 128), f32),
            jax.ShapeDtypeStruct((4, KEPT, depth), jnp.int32),
            jax.ShapeDtypeStruct((4, 8, depth), jnp.int32),
            jax.ShapeDtypeStruct((8, 128), jnp.int32),
            jax.ShapeDtypeStruct(node_coords.shape, f32),
            jax.ShapeDtypeStruct((4, 8, 16, depth), f32),
        ),
        in_specs=[hbm] * 5 + [pl.BlockSpec(memory_space=pltpu.SMEM)],
        out_specs=(vmem,) * 8,
        scratch_shapes=[
            pltpu.VMEM((2,) + control_points.shape, f32),
            pltpu.VMEM((8, 128), f32),
            pltpu.VMEM((9, 8, 128), f32),
            pltpu.VMEM((4, 8, 16, depth), f32),
            pltpu.VMEM((EARLY, 8, 128), f32),
            pltpu.SMEM(tiles.shape, jnp.int32),
            pltpu.SemaphoreType.DMA((5,)),
            pltpu.SemaphoreType.DMA((12,)),
            pltpu.SemaphoreType.DMA((12,)),
        ],
        compiler_params=pltpu.CompilerParams(
            collective_id=0, has_side_effects=True, vmem_limit_bytes=32 << 20
        ),
        name="gather",
    )(
        *(
            pltpu.with_memory_space_constraint(v, pltpu.HBM)
            for v in (node_coords, primitives, control_points, coefficients, tiles)
        ),
        counts,
    )


SPANS_EACH = 4


def motion_kernel(limits_ref, sorted_ref, index_ref, first_ref, x_ref, begun_ref, m_ref, table):
    scale = 1.0 / RADIUS
    tiles = sorted_ref.shape[2] // 128 - 1

    def part(at, carry):
        g, half, lanes, rows, pieces = part_of(at)
        number, most, top = (limits_ref[g, 3 * half + k] for k in range(3))
        few = most <= KEPT
        number = jnp.where(few, jnp.maximum(number - EARLY, 0), most)

        def fill(tiles):
            def some(i, carry):
                start = pl.multiple_of(EARLY + i * 8, 8)
                batch = index_ref[g, pl.ds(start, 8), lanes]
                for u in range(8):
                    index = jnp.broadcast_to(batch[u : u + 1], (8, 128))
                    table[i * 8 + u] = look_up(sorted_ref, g, index, tiles)
                return carry

            lax.fori_loop(0, (number + 7) // 8, some, 0)

        @pl.when(few & (top <= 128))
        def _():
            fill(1)

        @pl.when(few & (top > 128))
        def _():
            fill(tiles)

        @pl.when(most > KEPT)
        def _():
            first = first_ref[g, :, lanes]

            def some(i, carry):
                for u in range(BATCH):
                    at = i * BATCH + u
                    table[at] = look_up(sorted_ref, g, first + at, tiles)
                return carry

            lax.fori_loop(0, (number + BATCH - 1) // BATCH, some, 0)

        @pl.when(number > 0)
        def _():
            for spans in pieces:
                nodes = [x_ref[k, spans, rows, lanes] * scale for k in range(3)]
                total = tuple(m_ref[k, spans, rows, lanes] for k in range(3))
                total = add_points(table, (number + BATCH - 1) // BATCH, nodes, total)
                for k in range(3):
                    m_ref[k, spans, rows, lanes] = total[k]

        return carry

    lax.fori_loop(0, 8, part, 0)


def motion(limits, points, index, first, coords, begun):
    vmem = pl.BlockSpec(memory_space=pltpu.VMEM)
    smem = pl.BlockSpec(memory_space=pltpu.SMEM)
    return pl.pallas_call(
        motion_kernel,
        out_shape=jax.ShapeDtypeStruct(coords.shape, jnp.float32),
        in_specs=[smem] + [vmem] * 5,
        out_specs=vmem,
        scratch_shapes=[pltpu.VMEM((64 * SLOTS + 8, 8, 128), jnp.float32)],
        input_output_aliases={5: 0},
        compiler_params=pltpu.CompilerParams(vmem_limit_bytes=32 << 20),
        name="motion",
    )(limits, points, index, first, coords, begun)


def node_fields(coords, speed, state):
    rho, u, p = state[0], state[1:4], state[4]
    kinetic = 0.5 * rho * (u[0] * u[0] + u[1] * u[1] + u[2] * u[2])
    return dict(
        place=[a + b for a, b in zip(coords, speed)],
        speed=speed,
        u=u,
        p=p,
        amounts=[rho] + [rho * v for v in u] + [p / (GAMMA_GAS - 1.0) + kinetic],
        sound=jnp.sqrt(GAMMA_GAS * p / rho),
    )


def dot3(a, b):
    return a[0] * b[0] + a[1] * b[1] + a[2] * b[2]


def double_flux(left, right):
    edge = [b - a for a, b in zip(left["place"], right["place"])]
    magnitude = lax.rsqrt(dot3(edge, edge))
    inverse = magnitude * magnitude
    normal = [e * inverse for e in edge]
    frame = 0.5 * dot3([a + b for a, b in zip(left["speed"], right["speed"])], normal)
    left_un, right_un = dot3(left["u"], normal), dot3(right["u"], normal)
    left_rel, right_rel = left_un - frame, right_un - frame
    signal = jnp.maximum(
        jnp.abs(left_rel) + left["sound"] * magnitude,
        jnp.abs(right_rel) + right["sound"] * magnitude,
    )
    left_gain, right_gain = left_rel + signal, right_rel - signal
    flux = [a * left_gain + b * right_gain for a, b in zip(left["amounts"], right["amounts"])]
    pressure = left["p"] + right["p"]
    for k in range(3):
        flux[1 + k] = flux[1 + k] + pressure * normal[k]
    flux[4] = flux[4] + left["p"] * left_un + right["p"] * right_un
    return flux


def flux_kernel(
    x_ref,
    m_ref,
    q_ref,
    out_ref,
    landed,
    stage,
    send_sems,
    recv_sems,
):
    wait_all = meet(SIDES)
    length, chord_len, depth = x_ref.shape[1:]
    last = length - 1
    stage[0] = m_ref[:, 0]
    stage[1] = m_ref[:, last]
    stage[2] = m_ref[:, :, 0, :]
    stage[3] = m_ref[:, :, last, :]
    copies = []
    for side, offset in enumerate(SIDES):
        copy = pltpu.make_async_remote_copy(
            src_ref=stage.at[side],
            dst_ref=landed.at[side ^ 1],
            send_sem=send_sems.at[side],
            recv_sem=recv_sems.at[side ^ 1],
            device_id=peer(offset),
            device_id_type=MESH,
        )
        copies.append((copy, offset))

    step = 0.5 * SECTION_BETA

    def plane(s):
        return node_fields(
            [x_ref[k, s] for k in range(3)],
            [m_ref[k, s] for k in range(3)],
            [q_ref[k, s] for k in range(5)],
        )

    def moved(fields, axis):
        size = (chord_len, depth)[axis]

        def roll(v):
            return pltpu.roll(v, size - 1, axis=axis)

        return {
            name: [roll(v) for v in value] if isinstance(value, (list, tuple)) else roll(value)
            for name, value in fields.items()
        }

    row_at = lax.broadcasted_iota(jnp.int32, (chord_len, depth), 0)
    lane_at = lax.broadcasted_iota(jnp.int32, (chord_len, depth), 1)

    def inner(s, before):
        here = plane(s)
        ahead = plane(jnp.minimum(s + 1, last))
        span = double_flux(here, ahead)
        span = [jnp.where(s < last, f, 0.0) for f in span]
        chord = double_flux(here, moved(here, 0))
        chord = [jnp.where(row_at < chord_len - 1, f, 0.0) for f in chord]
        normal = double_flux(here, moved(here, 1))
        normal = [jnp.where(lane_at < depth - 1, f, 0.0) for f in normal]
        for k in range(5):
            residual = span[k] - before[k]
            residual = residual + (chord[k] - pltpu.roll(chord[k], 1, axis=0))
            residual = residual + (normal[k] - pltpu.roll(normal[k], 1, axis=1))
            out_ref[k, s] = here["amounts"][k] - step * residual
        return tuple(span)

    zero = jnp.zeros((chord_len, depth), jnp.float32)
    before = lax.fori_loop(0, AHEAD, inner, (zero,) * 5)
    wait_all()
    start_far_first(copies)
    lax.fori_loop(AHEAD, length, inner, before)
    wait_for(copies)


def section(node_coords, moved, primitives):
    depth = node_coords.shape[3]
    vmem = pl.BlockSpec(memory_space=pltpu.VMEM)
    f32 = jnp.float32
    return pl.pallas_call(
        flux_kernel,
        out_shape=(
            jax.ShapeDtypeStruct(primitives.shape, f32),
            jax.ShapeDtypeStruct((4, 3, 16, depth), f32),
        ),
        in_specs=[vmem] * 3,
        out_specs=(vmem,) * 2,
        scratch_shapes=[
            pltpu.VMEM((4, 3, 16, depth), f32),
            pltpu.SemaphoreType.DMA((4,)),
            pltpu.SemaphoreType.DMA((4,)),
        ],
        compiler_params=pltpu.CompilerParams(
            collective_id=1, has_side_effects=True, vmem_limit_bytes=32 << 20
        ),
        name="section",
    )(node_coords, moved, primitives)


def finish_kernel(
    x_ref, m_ref, q_ref, rims_ref, landed_ref, inner_ref, motion_hbm, state_hbm, rim_flux, out, sems
):
    length, chord_len, depth = x_ref.shape[1:]
    last = length - 1
    step = 0.5 * SECTION_BETA
    send_motion = pltpu.make_async_copy(m_ref, motion_hbm, sems.at[5])
    send_motion.start()
    for side, offset in enumerate(SIDES):
        row = last * (side % 2)
        sign = step if side % 2 == 0 else -step

        @pl.when(exists(offset))
        def _():
            def rim(ref, k):
                return ref[k, row] if side < 2 else ref[k, :, row, :]

            here = node_fields(
                [rim(x_ref, k) for k in range(3)],
                [rim(m_ref, k) for k in range(3)],
                [rim(q_ref, k) for k in range(5)],
            )
            there = node_fields(
                [rims_ref[side, k] for k in range(3)],
                [landed_ref[side, k] for k in range(3)],
                [rims_ref[side, 3 + k] for k in range(5)],
            )
            flux = double_flux(there, here) if side % 2 == 0 else double_flux(here, there)
            for k in range(5):
                rim_flux[side, k] = sign * flux[k]

        @pl.when(jnp.logical_not(exists(offset)))
        def _():
            rim_flux[side] = jnp.zeros(rim_flux.shape[1:], jnp.float32)

    row_at = lax.broadcasted_iota(jnp.int32, (chord_len, depth), 0)
    sends = []
    for k in range(5):
        for s in range(length):
            low = jnp.where(row_at == 0, rim_flux[2, k, s : s + 1], 0.0)
            value = inner_ref[k, s] + jnp.where(row_at == last, rim_flux[3, k, s : s + 1], low)
            if s == 0:
                value = value + rim_flux[0, k]
            if s == last:
                value = value + rim_flux[1, k]
            out[k, s] = value
        sends.append(pltpu.make_async_copy(out.at[k], state_hbm.at[k], sems.at[k]))
        sends[-1].start()
    for sent in sends + [send_motion]:
        sent.wait()


def finish(coords, moved, states, rims, landed, inner):
    vmem = pl.BlockSpec(memory_space=pltpu.VMEM)
    hbm = pl.BlockSpec(memory_space=pltpu.HBM)
    f32 = jnp.float32
    return pl.pallas_call(
        finish_kernel,
        out_shape=(pltpu.HBM(moved.shape, f32), pltpu.HBM(states.shape, f32)),
        in_specs=[vmem] * 6,
        out_specs=(hbm, hbm),
        scratch_shapes=[
            pltpu.VMEM((4, 5, 16, coords.shape[3]), f32),
            pltpu.VMEM(states.shape, f32),
            pltpu.SemaphoreType.DMA((6,)),
        ],
        compiler_params=pltpu.CompilerParams(vmem_limit_bytes=32 << 20),
        name="finish",
    )(coords, moved, states, rims, landed, inner)


def body(node_coords, primitives, control_points, coefficients, support_tiles, support_counts):
    coords, states, points, index, first, limits, begun, rims = gather(
        node_coords, primitives, control_points, coefficients, support_tiles, support_counts
    )
    moved = motion(limits, points, index, first, coords, begun)
    inner, landed = section(coords, moved, states)
    return finish(coords, moved, states, rims, landed, inner)


def solution(mesh):
    in_specs = (
        P(None, "span", "chord", None),
        P(None, "span", "chord", None),
        P(None, ("span", "chord"), None),
        P(None, ("span", "chord"), None),
        P("span", "chord", None),
        P("span", "chord"),
    )
    out_specs = (P(None, "span", "chord", None), P(None, "span", "chord", None))
    return jax.shard_map(body, mesh=mesh, in_specs=in_specs, out_specs=out_specs, check_vma=False)
```

```python
import jax
import jax.numpy as jnp
from jax import lax
from jax.experimental import pallas as pl
from jax.experimental.pallas import tpu as pltpu
from jax.sharding import PartitionSpec as P

RADIUS = 12
GAMMA_GAS = 1.4
SECTION_BETA = 0.2
SLOTS = 6
BATCH = 4
KEPT = 32
EARLY = 8
OWN_KEPT = 16
OWN = 12
AHEAD = 4
NOWHERE = 511 * 64
REACH = 1.001
MESH = pl.DeviceIdType.MESH
AROUND = tuple((a, b) for a in (-1, 0, 1) for b in (-1, 0, 1) if (a, b) != (0, 0))
SIDES = ((-1, 0), (1, 0), (0, -1), (0, 1))


def peer(offset):
    spans, chords = lax.axis_size("span"), lax.axis_size("chord")
    return {
        "span": lax.rem(lax.axis_index("span") + offset[0] + spans, spans),
        "chord": lax.rem(lax.axis_index("chord") + offset[1] + chords, chords),
    }


def exists(offset):
    a = lax.axis_index("span") + offset[0]
    b = lax.axis_index("chord") + offset[1]
    return (a >= 0) & (a < lax.axis_size("span")) & (b >= 0) & (b < lax.axis_size("chord"))


def opposite(offset):
    return (-offset[0], -offset[1])


def meet(offsets):
    barrier = pltpu.get_barrier_semaphore()
    for offset in offsets:

        @pl.when(exists(offset))
        def _():
            pl.semaphore_signal(barrier, inc=1, device_id=peer(offset), device_id_type=MESH)

    number = sum(jnp.where(exists(offset), 1, 0) for offset in offsets)
    return lambda: pl.semaphore_wait(barrier, number)


def wait_for(copies):
    for copy, offset in copies:

        @pl.when(exists(offset))
        def _():
            copy.wait_send()

        @pl.when(exists(opposite(offset)))
        def _():
            copy.wait_recv()


def look_up(sorted_ref, g, index, tiles):
    found = jnp.zeros((8, 128), jnp.float32)
    for j in range(tiles):
        more = sorted_ref[g, :, 128 * j : 128 * j + 128]
        more = jnp.take_along_axis(more, index & 127, axis=1)
        found = jnp.where(index >> 7 == j, more, found)
    return found


def add_points(table, steps, nodes, total):
    x, y, z = nodes

    def step(i, total):
        total = list(total)
        for u in range(BATCH):
            point = [table[i * BATCH + u, v : v + 1, :] for v in range(6)]
            dx, dy, dz = x - point[0], y - point[1], z - point[2]
            squared = jnp.maximum(dx * dx + dy * dy + dz * dz, 1e-30)
            remain = jnp.maximum(1.0 - squared * lax.rsqrt(squared), 0.0)
            second = remain * remain
            weight = second * second * (1.25 - remain)
            for k in range(3):
                total[k] = total[k] + point[3 + k] * weight
        return tuple(total)

    return lax.fori_loop(0, steps, step, total)


def part_of(at):
    g, half = at // 2, at % 2
    lanes = pl.ds(pl.multiple_of(half * 128, 128), 128)
    rows = pl.ds(pl.multiple_of(g % 2 * 8, 8), 8)
    pieces = [pl.ds(g // 2 * 8 + k * SPANS_EACH, SPANS_EACH) for k in range(8 // SPANS_EACH)]
    return g, half, lanes, rows, pieces


def start_far_first(copies):
    core = lax.rem(lax.axis_index("chord"), 2)
    for side, wanted in ((2, core == 0), (3, core == 1), (0, True), (1, True), (3, core == 0), (2, core == 1)):
        copy, offset = copies[side]

        @pl.when(exists(offset) & wanted)
        def _():
            copy.start()


def add_listed(sorted_ref, index_ref, table, x_ref, start_ref, out_ref, number):
    tiles = sorted_ref.shape[2] // 128

    def part(at, carry):
        g, half, lanes, rows, pieces = part_of(at)
        for i in range(0, number, 8):
            batch = index_ref[g, i : i + 8, lanes]
            for u in range(8):
                index = jnp.broadcast_to(batch[u : u + 1], (8, 128))
                table[i + u] = look_up(sorted_ref, g, index, tiles)
        for spans in pieces:
            nodes = [x_ref[k, spans, rows, lanes] * (1.0 / RADIUS) for k in range(3)]
            if start_ref is None:
                total = (jnp.zeros_like(nodes[0]),) * 3
            else:
                total = tuple(start_ref[k, spans, rows, lanes] for k in range(3))
            total = add_points(table, number // BATCH, nodes, total)
            for k in range(3):
                out_ref[k, spans, rows, lanes] = total[k]
        return carry

    lax.fori_loop(0, 8, part, 0)


def flags(mask):
    return jnp.where(mask, 1.0, 0.0).astype(jnp.bfloat16)


def build_lists(values, useds, drops, boxes, z_low, z_high, kept):
    groups, depth = len(values), z_low.shape[1]
    row_at = lax.broadcasted_iota(jnp.int32, (8, 128), 0)
    big_lane = lax.broadcasted_iota(jnp.int32, (128, 128), 1)
    big_row = lax.broadcasted_iota(jnp.int32, (128, 128), 0)
    blank = jnp.zeros((4, 128), jnp.float32)
    keys, keeps, reaches = [], [], []
    for value, used, drop in zip(values, useds, drops):
        keys.append(value[2:3])
        apart = []
        for axis in range(2):
            along = value[axis : axis + 1]
            gaps = [jnp.maximum(jnp.maximum(b[0] - along, along - b[1]), 0.0) for b in boxes[axis]]
            apart.append([gap * gap for gap in gaps])
        spare = [REACH * REACH - apart[0][h] - apart[1][c] for h in range(2) for c in range(2)]
        spare = jnp.concatenate(spare + [blank], axis=0)
        near = (spare > 0.0) & used & (row_at < 4)
        keep = jnp.where(near, 1.0, 0.0)
        if drop is not None:
            keep = jnp.where(drop > 0.5, 0.0, keep)
        keeps.append(keep)
        reaches.append(jnp.where(near, jnp.sqrt(jnp.maximum(spare, 0.0)) * 1.01 + 0.01, 0.0))
    doubled = [jnp.concatenate([k, jnp.zeros_like(k)], axis=0).astype(jnp.bfloat16) for k in keeps]

    columns = [jnp.broadcast_to(key, (128, 128)).T for key in keys]

    def counted(blocks):
        return sum(
            jnp.dot(keep, block, preferred_element_type=jnp.float32)
            for keep, block in zip(doubled, blocks)
        )

    ahead = []
    for j in range(groups):
        row = []
        for i in range(groups):
            if j < i:
                before = columns[j] <= keys[i]
            elif j > i:
                before = columns[j] < keys[i]
            else:
                before = (columns[j] < keys[i]) | ((columns[j] == keys[i]) & (big_row < big_lane))
            row.append(flags(before))
        ahead.append(jnp.concatenate(row, axis=1))
    rank = counted(ahead)
    wide = [jnp.concatenate([c] * (depth // 128), axis=1) for c in columns]
    first = counted([flags(c < z_low - REACH) for c in wide])
    final = counted([flags(c <= z_high + REACH) for c in wide])

    parts = []
    for value, reach in zip(values, reaches):
        one = value.astype(jnp.bfloat16).astype(jnp.float32)
        rest = value - one
        two = rest.astype(jnp.bfloat16).astype(jnp.float32)
        three = rest - two
        parts.append(jnp.concatenate([one, two, three, reach], axis=0).astype(jnp.bfloat16))
    order = big_row.astype(jnp.float32)
    step_at = lax.broadcasted_iota(jnp.int32, (kept, depth), 0)
    lower = lax.broadcasted_iota(jnp.int32, (kept, kept), 0) > lax.broadcasted_iota(
        jnp.int32, (kept, kept), 1
    )
    lists = []
    for g in range(4):
        total = jnp.zeros((32, 128 * groups), jnp.float32)
        for i in range(groups):
            keep = keeps[i][g : g + 1] > 0.5
            at = jnp.where(keep, rank[g : g + 1, 128 * i : 128 * i + 128], -1.0)
            place = jnp.concatenate([flags(at == order + 128.0 * j) for j in range(groups)], axis=0)
            total = total + lax.dot_general(
                parts[i], place, (((1,), (1,)), ((), ())), preferred_element_type=jnp.float32
            )
        listed = total[0:8] + total[8:16] + total[16:24]
        start = first[g : g + 1].astype(jnp.int32)
        index = step_at + start
        bound = final[g : g + 1].astype(jnp.int32)

        def looked(row):
            tiles = [jnp.broadcast_to(row[:, 128 * j : 128 * j + 128], (8, 128)) for j in range(groups)]
            rows = []
            for k in range(kept // 8):
                cols = []
                for h in range(depth // 128):
                    want = index[8 * k : 8 * k + 8, 128 * h : 128 * h + 128]
                    found = jnp.zeros((8, 128), jnp.float32)
                    for j, tile in enumerate(tiles):
                        more = jnp.take_along_axis(tile, want & 127, axis=1)
                        found = jnp.where(want >> 7 == j, more, found)
                    cols.append(found)
                rows.append(jnp.concatenate(cols, axis=1))
            return jnp.concatenate(rows, axis=0)

        z = looked(listed[2:3])
        reach = looked(total[24 + g : 25 + g])
        inside = (index < bound) & (z > z_low - reach) & (z < z_high + reach)
        skipped = jnp.dot(
            flags(lower), flags(jnp.logical_not(inside)), preferred_element_type=jnp.float32
        )
        code = jnp.where(inside, index * 64 + skipped.astype(jnp.int32), NOWHERE)
        shift = 1
        while shift < kept:
            later = pltpu.roll(code, kept - shift, axis=0)
            left = jnp.where((code & shift) != 0, NOWHERE, code)
            code = jnp.where(((later & shift) != 0) & (step_at < kept - shift), later, left)
            shift = 2 * shift
        number = jnp.sum(jnp.where(inside, 1, 0), axis=0, keepdims=True)
        lists.append((listed, code >> 6, number, start, bound))
    return lists


def gather_kernel(
    x_hbm,
    q_hbm,
    points_hbm,
    coef_hbm,
    tiles_hbm,
    count_ref,
    x_v,
    q_v,
    sorted_ref,
    index_ref,
    first_ref,
    limits_ref,
    part_ref,
    rims_ref,
    tile_v,
    own,
    window,
    stage,
    table,
    own_sorted,
    own_index,
    fits_ref,
    tiles_ref,
    local_sems,
    send_sems,
    recv_sems,
):
    window[...] = jnp.zeros_like(window)
    wait_all = meet(AROUND)
    fetches = []
    for src, dst in (
        (points_hbm, tile_v.at[0]),
        (coef_hbm, tile_v.at[1]),
        (tiles_hbm, tiles_ref),
        (x_hbm, x_v),
        (q_hbm, q_v),
    ):
        fetch = pltpu.make_async_copy(src, dst, local_sems.at[len(fetches)])
        fetch.start()
        fetches.append(fetch)
    fetches[0].wait()
    fetches[1].wait()

    scale = 1.0 / RADIUS
    own[...] = jnp.zeros_like(own)
    for half in range(2):
        lanes = pl.ds(64 * half, 64)
        own[0:3, lanes] = tile_v[0, :, 0, :] * scale
        own[3:6, lanes] = tile_v[1, :, 0, :] * 4.0

    length = x_v.shape[1]
    span_at, chord_at = lax.axis_index("span"), lax.axis_index("chord")
    chords = lax.axis_size("chord")
    lane = lax.broadcasted_iota(jnp.int32, (8, 128), 1)
    row_at = lax.broadcasted_iota(jnp.int32, (8, 128), 0)

    def prepare():
        for fetch in fetches[2:]:
            fetch.wait()
        for side, row in ((2, 0), (3, length - 1)):
            stage[side, 0:3] = x_v[:, :, row, :]
            stage[side, 3:8] = q_v[:, :, row, :]
        for side, row in ((0, 0), (1, length - 1)):
            stage[side, 0:3] = x_v[:, row]
            stage[side, 3:8] = q_v[:, row]

    def bounds(block):
        low = jnp.min(jnp.min(block, axis=0), axis=0, keepdims=True) * scale
        high = jnp.max(jnp.max(block, axis=0), axis=0, keepdims=True) * scale
        return low, high

    def interval(block):
        low, high = bounds(block)
        return jnp.min(low, axis=1, keepdims=True), jnp.max(high, axis=1, keepdims=True)

    def all_bounds():
        boxes = (
            [interval(x_v[0, 8 * h : 8 * h + 8]) for h in range(2)],
            [interval(x_v[1, :, 8 * c : 8 * c + 8]) for c in range(2)],
        )
        return boxes, *bounds(x_v[2])

    def place_of(slot):
        tile = tiles_ref[0, 0, slot]
        at = (tile // chords - span_at + 1) * 3 + (tile % chords - chord_at + 1)
        return jnp.where(slot < count_ref[0, 0], jnp.clip(at, 0, 8), 9)

    def take_own():
        own_used = sum(jnp.where(place_of(slot) == 4, 1, 0) for slot in range(SLOTS)) > 0
        lists = build_lists([own[...]], [lane < 64], [None], *all_bounds(), OWN_KEPT)
        fits = []
        for g, (listed, index, number, start, bound) in enumerate(lists):
            own_sorted[g] = listed
            fit = (jnp.max(number, axis=1, keepdims=True) <= OWN) & (
                jnp.max(bound - start, axis=1, keepdims=True) <= OWN_KEPT
            )
            own_index[g] = jnp.where(fit & own_used, index, NOWHERE >> 6)
            fits.append(jnp.broadcast_to(jnp.where(fit, 1.0, 0.0), (1, 128)))
        fits_ref[...] = jnp.concatenate(fits + [jnp.zeros((4, 128), jnp.float32)], axis=0)
        add_listed(own_sorted, own_index, table, x_v, None, part_ref, OWN)

    ahead = lax.rem(chord_at, 4) < 2

    @pl.when(ahead)
    def _():
        prepare()
        take_own()

    wait_all()

    copies = []

    def remote(src, dst, offset):
        at = len(copies)
        copy = pltpu.make_async_remote_copy(
            src_ref=src,
            dst_ref=dst,
            send_sem=send_sems.at[at],
            recv_sem=recv_sems.at[at],
            device_id=peer(offset),
            device_id_type=MESH,
        )
        copies.append((copy, offset))

    for a, b in AROUND:
        remote(own, window.at[(1 - a) * 3 + 1 - b], (a, b))
        pl.when(exists((a, b)))(copies[-1][0].start)
    window[4] = own[...]
    pl.when(jnp.logical_not(ahead))(prepare)
    for side, offset in enumerate(SIDES):
        remote(stage.at[side], rims_ref.at[side ^ 1], offset)
    start_far_first(copies[8:])
    pl.when(jnp.logical_not(ahead))(take_own)
    boxes, z_low, z_high = all_bounds()
    places = [place_of(slot) for slot in range(SLOTS)]
    fits = fits_ref[...]

    wait_for(copies[:8])
    values, useds, drops = [], [], []
    for pair in range(SLOTS // 2):
        left, right = places[2 * pair], places[2 * pair + 1]
        value = jnp.where(
            lane < 64, window[jnp.where(left > 8, 4, left)], window[jnp.where(right > 8, 4, right)]
        )
        place = jnp.where(lane < 64, left, right)
        useds.append(place <= 8)
        drops.append(jnp.where(place == 4, fits, 0.0))
        values.append(jnp.where((row_at >= 3) & (place > 8), 0.0, value))
    lists = build_lists(values, useds, drops, boxes, z_low, z_high, KEPT)
    limits = jnp.zeros((8, 128), jnp.int32)
    for g, (listed, index, number, start, bound) in enumerate(lists):
        sorted_ref[g] = listed
        first_ref[g] = jnp.broadcast_to(start, first_ref.shape[1:])
        for h in range(index.shape[1] // 128):
            cut = slice(128 * h, 128 * h + 128)
            most = jnp.max((bound - start)[:, cut], axis=1, keepdims=True)
            index_ref[g, :, cut] = jnp.where(most <= KEPT, index[:, cut], NOWHERE >> 6)
            found = (
                jnp.max(number[:, cut], axis=1, keepdims=True),
                most,
                jnp.max(bound[:, cut], axis=1, keepdims=True),
            )
            for i, limit in enumerate(found):
                limits = jnp.where((row_at == g) & (lane == 3 * h + i), limit, limits)
    limits_ref[...] = limits
    add_listed(sorted_ref, index_ref, table, x_v, part_ref, part_ref, EARLY)
    wait_for(copies[8:])


def gather(node_coords, primitives, control_points, coefficients, tiles, counts):
    depth = node_coords.shape[3]
    vmem = pl.BlockSpec(memory_space=pltpu.VMEM)
    hbm = pl.BlockSpec(memory_space=pltpu.HBM)
    f32 = jnp.float32
    return pl.pallas_call(
        gather_kernel,
        out_shape=(
            jax.ShapeDtypeStruct(node_coords.shape, f32),
            jax.ShapeDtypeStruct(primitives.shape, f32),
            jax.ShapeDtypeStruct((4, 8, 64 * SLOTS), f32),
            jax.ShapeDtypeStruct((4, KEPT, depth), jnp.int32),
            jax.ShapeDtypeStruct((4, 8, depth), jnp.int32),
            jax.ShapeDtypeStruct((8, 128), jnp.int32),
            jax.ShapeDtypeStruct(node_coords.shape, f32),
            jax.ShapeDtypeStruct((4, 8, 16, depth), f32),
        ),
        in_specs=[hbm] * 5 + [pl.BlockSpec(memory_space=pltpu.SMEM)],
        out_specs=(vmem,) * 8,
        scratch_shapes=[
            pltpu.VMEM((2,) + control_points.shape, f32),
            pltpu.VMEM((8, 128), f32),
            pltpu.VMEM((9, 8, 128), f32),
            pltpu.VMEM((4, 8, 16, depth), f32),
            pltpu.VMEM((OWN_KEPT, 8, 128), f32),
            pltpu.VMEM((4, 8, 128), f32),
            pltpu.VMEM((4, OWN_KEPT, depth), jnp.int32),
            pltpu.VMEM((8, 128), f32),
            pltpu.SMEM(tiles.shape, jnp.int32),
            pltpu.SemaphoreType.DMA((5,)),
            pltpu.SemaphoreType.DMA((12,)),
            pltpu.SemaphoreType.DMA((12,)),
        ],
        compiler_params=pltpu.CompilerParams(
            collective_id=0, has_side_effects=True, vmem_limit_bytes=32 << 20
        ),
        name="gather",
    )(
        *(
            pltpu.with_memory_space_constraint(v, pltpu.HBM)
            for v in (node_coords, primitives, control_points, coefficients, tiles)
        ),
        counts,
    )


SPANS_EACH = 4


def motion_kernel(limits_ref, sorted_ref, index_ref, first_ref, x_ref, begun_ref, m_ref, table):
    scale = 1.0 / RADIUS
    tiles = sorted_ref.shape[2] // 128

    def part(at, carry):
        g, half, lanes, rows, pieces = part_of(at)
        number, most, top = (limits_ref[g, 3 * half + k] for k in range(3))
        few = most <= KEPT
        number = jnp.where(few, jnp.maximum(number - EARLY, 0), most)

        def fill(tiles):
            def some(i, carry):
                start = pl.multiple_of(EARLY + i * 8, 8)
                batch = index_ref[g, pl.ds(start, 8), lanes]
                for u in range(8):
                    index = jnp.broadcast_to(batch[u : u + 1], (8, 128))
                    table[i * 8 + u] = look_up(sorted_ref, g, index, tiles)
                return carry

            lax.fori_loop(0, (number + 7) // 8, some, 0)

        @pl.when(few & (top <= 128))
        def _():
            fill(1)

        @pl.when(few & (top > 128))
        def _():
            fill(tiles)

        @pl.when(most > KEPT)
        def _():
            first = first_ref[g, :, lanes]

            def some(i, carry):
                for u in range(BATCH):
                    at = i * BATCH + u
                    table[at] = look_up(sorted_ref, g, first + at, tiles)
                return carry

            lax.fori_loop(0, (number + BATCH - 1) // BATCH, some, 0)

        @pl.when(number > 0)
        def _():
            for spans in pieces:
                nodes = [x_ref[k, spans, rows, lanes] * scale for k in range(3)]
                total = tuple(m_ref[k, spans, rows, lanes] for k in range(3))
                total = add_points(table, (number + BATCH - 1) // BATCH, nodes, total)
                for k in range(3):
                    m_ref[k, spans, rows, lanes] = total[k]

        return carry

    lax.fori_loop(0, 8, part, 0)


def motion(limits, points, index, first, coords, begun):
    vmem = pl.BlockSpec(memory_space=pltpu.VMEM)
    smem = pl.BlockSpec(memory_space=pltpu.SMEM)
    return pl.pallas_call(
        motion_kernel,
        out_shape=jax.ShapeDtypeStruct(coords.shape, jnp.float32),
        in_specs=[smem] + [vmem] * 5,
        out_specs=vmem,
        scratch_shapes=[pltpu.VMEM((64 * SLOTS + 8, 8, 128), jnp.float32)],
        input_output_aliases={5: 0},
        compiler_params=pltpu.CompilerParams(vmem_limit_bytes=32 << 20),
        name="motion",
    )(limits, points, index, first, coords, begun)


def node_fields(coords, speed, state):
    rho, u, p = state[0], state[1:4], state[4]
    kinetic = 0.5 * rho * (u[0] * u[0] + u[1] * u[1] + u[2] * u[2])
    return dict(
        place=[a + b for a, b in zip(coords, speed)],
        speed=speed,
        u=u,
        p=p,
        amounts=[rho] + [rho * v for v in u] + [p / (GAMMA_GAS - 1.0) + kinetic],
        sound=jnp.sqrt(GAMMA_GAS * p / rho),
    )


def dot3(a, b):
    return a[0] * b[0] + a[1] * b[1] + a[2] * b[2]


def double_flux(left, right):
    edge = [b - a for a, b in zip(left["place"], right["place"])]
    magnitude = lax.rsqrt(dot3(edge, edge))
    inverse = magnitude * magnitude
    normal = [e * inverse for e in edge]
    frame = 0.5 * dot3([a + b for a, b in zip(left["speed"], right["speed"])], normal)
    left_un, right_un = dot3(left["u"], normal), dot3(right["u"], normal)
    left_rel, right_rel = left_un - frame, right_un - frame
    signal = jnp.maximum(
        jnp.abs(left_rel) + left["sound"] * magnitude,
        jnp.abs(right_rel) + right["sound"] * magnitude,
    )
    left_gain, right_gain = left_rel + signal, right_rel - signal
    flux = [a * left_gain + b * right_gain for a, b in zip(left["amounts"], right["amounts"])]
    pressure = left["p"] + right["p"]
    for k in range(3):
        flux[1 + k] = flux[1 + k] + pressure * normal[k]
    flux[4] = flux[4] + left["p"] * left_un + right["p"] * right_un
    return flux


def flux_kernel(
    x_ref,
    m_ref,
    q_ref,
    out_ref,
    landed,
    stage,
    send_sems,
    recv_sems,
):
    wait_all = meet(SIDES)
    length, chord_len, depth = x_ref.shape[1:]
    last = length - 1
    stage[0] = m_ref[:, 0]
    stage[1] = m_ref[:, last]
    stage[2] = m_ref[:, :, 0, :]
    stage[3] = m_ref[:, :, last, :]
    copies = []
    for side, offset in enumerate(SIDES):
        copy = pltpu.make_async_remote_copy(
            src_ref=stage.at[side],
            dst_ref=landed.at[side ^ 1],
            send_sem=send_sems.at[side],
            recv_sem=recv_sems.at[side ^ 1],
            device_id=peer(offset),
            device_id_type=MESH,
        )
        copies.append((copy, offset))

    step = 0.5 * SECTION_BETA

    def plane(s):
        return node_fields(
            [x_ref[k, s] for k in range(3)],
            [m_ref[k, s] for k in range(3)],
            [q_ref[k, s] for k in range(5)],
        )

    def moved(fields, axis):
        size = (chord_len, depth)[axis]

        def roll(v):
            return pltpu.roll(v, size - 1, axis=axis)

        return {
            name: [roll(v) for v in value] if isinstance(value, (list, tuple)) else roll(value)
            for name, value in fields.items()
        }

    row_at = lax.broadcasted_iota(jnp.int32, (chord_len, depth), 0)
    lane_at = lax.broadcasted_iota(jnp.int32, (chord_len, depth), 1)

    def inner(s, before):
        here = plane(s)
        ahead = plane(jnp.minimum(s + 1, last))
        span = double_flux(here, ahead)
        span = [jnp.where(s < last, f, 0.0) for f in span]
        chord = double_flux(here, moved(here, 0))
        chord = [jnp.where(row_at < chord_len - 1, f, 0.0) for f in chord]
        normal = double_flux(here, moved(here, 1))
        normal = [jnp.where(lane_at < depth - 1, f, 0.0) for f in normal]
        for k in range(5):
            residual = span[k] - before[k]
            residual = residual + (chord[k] - pltpu.roll(chord[k], 1, axis=0))
            residual = residual + (normal[k] - pltpu.roll(normal[k], 1, axis=1))
            out_ref[k, s] = here["amounts"][k] - step * residual
        return tuple(span)

    zero = jnp.zeros((chord_len, depth), jnp.float32)
    before = lax.fori_loop(0, AHEAD, inner, (zero,) * 5)
    wait_all()
    start_far_first(copies)
    lax.fori_loop(AHEAD, length, inner, before)
    wait_for(copies)


def section(node_coords, moved, primitives):
    depth = node_coords.shape[3]
    vmem = pl.BlockSpec(memory_space=pltpu.VMEM)
    f32 = jnp.float32
    return pl.pallas_call(
        flux_kernel,
        out_shape=(
            jax.ShapeDtypeStruct(primitives.shape, f32),
            jax.ShapeDtypeStruct((4, 3, 16, depth), f32),
        ),
        in_specs=[vmem] * 3,
        out_specs=(vmem,) * 2,
        scratch_shapes=[
            pltpu.VMEM((4, 3, 16, depth), f32),
            pltpu.SemaphoreType.DMA((4,)),
            pltpu.SemaphoreType.DMA((4,)),
        ],
        compiler_params=pltpu.CompilerParams(
            collective_id=1, has_side_effects=True, vmem_limit_bytes=32 << 20
        ),
        name="section",
    )(node_coords, moved, primitives)


def finish_kernel(
    x_ref, m_ref, q_ref, rims_ref, landed_ref, inner_ref, motion_hbm, state_hbm, rim_flux, out, sems
):
    length, chord_len, depth = x_ref.shape[1:]
    last = length - 1
    step = 0.5 * SECTION_BETA
    send_motion = pltpu.make_async_copy(m_ref, motion_hbm, sems.at[5])
    send_motion.start()
    for side, offset in enumerate(SIDES):
        row = last * (side % 2)
        sign = step if side % 2 == 0 else -step

        @pl.when(exists(offset))
        def _():
            def rim(ref, k):
                return ref[k, row] if side < 2 else ref[k, :, row, :]

            here = node_fields(
                [rim(x_ref, k) for k in range(3)],
                [rim(m_ref, k) for k in range(3)],
                [rim(q_ref, k) for k in range(5)],
            )
            there = node_fields(
                [rims_ref[side, k] for k in range(3)],
                [landed_ref[side, k] for k in range(3)],
                [rims_ref[side, 3 + k] for k in range(5)],
            )
            flux = double_flux(there, here) if side % 2 == 0 else double_flux(here, there)
            for k in range(5):
                rim_flux[side, k] = sign * flux[k]

        @pl.when(jnp.logical_not(exists(offset)))
        def _():
            rim_flux[side] = jnp.zeros(rim_flux.shape[1:], jnp.float32)

    row_at = lax.broadcasted_iota(jnp.int32, (chord_len, depth), 0)
    sends = []
    for k in range(5):
        for s in range(length):
            low = jnp.where(row_at == 0, rim_flux[2, k, s : s + 1], 0.0)
            value = inner_ref[k, s] + jnp.where(row_at == last, rim_flux[3, k, s : s + 1], low)
            if s == 0:
                value = value + rim_flux[0, k]
            if s == last:
                value = value + rim_flux[1, k]
            out[k, s] = value
        sends.append(pltpu.make_async_copy(out.at[k], state_hbm.at[k], sems.at[k]))
        sends[-1].start()
    for sent in sends + [send_motion]:
        sent.wait()


def finish(coords, moved, states, rims, landed, inner):
    vmem = pl.BlockSpec(memory_space=pltpu.VMEM)
    hbm = pl.BlockSpec(memory_space=pltpu.HBM)
    f32 = jnp.float32
    return pl.pallas_call(
        finish_kernel,
        out_shape=(pltpu.HBM(moved.shape, f32), pltpu.HBM(states.shape, f32)),
        in_specs=[vmem] * 6,
        out_specs=(hbm, hbm),
        scratch_shapes=[
            pltpu.VMEM((4, 5, 16, coords.shape[3]), f32),
            pltpu.VMEM(states.shape, f32),
            pltpu.SemaphoreType.DMA((6,)),
        ],
        compiler_params=pltpu.CompilerParams(vmem_limit_bytes=32 << 20),
        name="finish",
    )(coords, moved, states, rims, landed, inner)


def body(node_coords, primitives, control_points, coefficients, support_tiles, support_counts):
    coords, states, points, index, first, limits, begun, rims = gather(
        node_coords, primitives, control_points, coefficients, support_tiles, support_counts
    )
    moved = motion(limits, points, index, first, coords, begun)
    inner, landed = section(coords, moved, states)
    return finish(coords, moved, states, rims, landed, inner)


def solution(mesh):
    in_specs = (
        P(None, "span", "chord", None),
        P(None, "span", "chord", None),
        P(None, ("span", "chord"), None),
        P(None, ("span", "chord"), None),
        P("span", "chord", None),
        P("span", "chord"),
    )
    out_specs = (P(None, "span", "chord", None), P(None, "span", "chord", None))
    return jax.shard_map(body, mesh=mesh, in_specs=in_specs, out_specs=out_specs, check_vma=False)
```

```python
import jax
import jax.numpy as jnp
from jax import lax
from jax.experimental import pallas as pl
from jax.experimental.pallas import tpu as pltpu
from jax.sharding import PartitionSpec as P

RADIUS = 12
GAMMA_GAS = 1.4
SECTION_BETA = 0.2
SLOTS = 6
BATCH = 4
KEPT = 32
EARLY = 8
OWN_KEPT = 16
OWN = 12
AHEAD = 4
NOWHERE = 511 * 64
REACH = 1.001
MESH = pl.DeviceIdType.MESH
AROUND = tuple((a, b) for a in (-1, 0, 1) for b in (-1, 0, 1) if (a, b) != (0, 0))
SIDES = ((-1, 0), (1, 0), (0, -1), (0, 1))


def peer(offset):
    spans, chords = lax.axis_size("span"), lax.axis_size("chord")
    return {
        "span": lax.rem(lax.axis_index("span") + offset[0] + spans, spans),
        "chord": lax.rem(lax.axis_index("chord") + offset[1] + chords, chords),
    }


def exists(offset):
    a = lax.axis_index("span") + offset[0]
    b = lax.axis_index("chord") + offset[1]
    return (a >= 0) & (a < lax.axis_size("span")) & (b >= 0) & (b < lax.axis_size("chord"))


def opposite(offset):
    return (-offset[0], -offset[1])


def meet(offsets):
    barrier = pltpu.get_barrier_semaphore()
    for offset in offsets:

        @pl.when(exists(offset))
        def _():
            pl.semaphore_signal(barrier, inc=1, device_id=peer(offset), device_id_type=MESH)

    number = sum(jnp.where(exists(offset), 1, 0) for offset in offsets)
    return lambda: pl.semaphore_wait(barrier, number)


def wait_for(copies):
    for copy, offset in copies:

        @pl.when(exists(offset))
        def _():
            copy.wait_send()

        @pl.when(exists(opposite(offset)))
        def _():
            copy.wait_recv()


def look_up(sorted_ref, g, index, tiles):
    found = jnp.zeros((8, 128), jnp.float32)
    for j in range(tiles):
        more = sorted_ref[g, :, 128 * j : 128 * j + 128]
        more = jnp.take_along_axis(more, index & 127, axis=1)
        found = jnp.where(index >> 7 == j, more, found)
    return found


def add_points(table, steps, nodes, total):
    x, y, z = nodes

    def step(i, total):
        total = list(total)
        for u in range(BATCH):
            point = [table[i * BATCH + u, v : v + 1, :] for v in range(6)]
            dx, dy, dz = x - point[0], y - point[1], z - point[2]
            squared = jnp.maximum(dx * dx + dy * dy + dz * dz, 1e-30)
            remain = jnp.maximum(1.0 - squared * lax.rsqrt(squared), 0.0)
            second = remain * remain
            weight = second * second * (1.25 - remain)
            for k in range(3):
                total[k] = total[k] + point[3 + k] * weight
        return tuple(total)

    return lax.fori_loop(0, steps, step, total)


def part_of(at):
    g, half = at // 2, at % 2
    lanes = pl.ds(pl.multiple_of(half * 128, 128), 128)
    rows = pl.ds(pl.multiple_of(g % 2 * 8, 8), 8)
    pieces = [pl.ds(g // 2 * 8 + k * SPANS_EACH, SPANS_EACH) for k in range(8 // SPANS_EACH)]
    return g, half, lanes, rows, pieces


def start_far_first(copies):
    core = lax.rem(lax.axis_index("chord"), 2)
    x = lax.rem(lax.axis_index("span"), 4)
    turns = (
        (0, x == 0),
        (1, x == 3),
        (2, core == 0),
        (3, core == 1),
        (0, x != 0),
        (1, x != 3),
        (3, core == 0),
        (2, core == 1),
    )
    for side, wanted in turns:
        copy, offset = copies[side]

        @pl.when(exists(offset) & wanted)
        def _():
            copy.start()


def add_listed(sorted_ref, index_ref, table, x_ref, start_ref, out_ref, number):
    tiles = sorted_ref.shape[2] // 128

    def part(at, carry):
        g, half, lanes, rows, pieces = part_of(at)
        for i in range(0, number, 8):
            batch = index_ref[g, i : i + 8, lanes]
            for u in range(8):
                index = jnp.broadcast_to(batch[u : u + 1], (8, 128))
                table[i + u] = look_up(sorted_ref, g, index, tiles)
        for spans in pieces:
            nodes = [x_ref[k, spans, rows, lanes] * (1.0 / RADIUS) for k in range(3)]
            if start_ref is None:
                total = (jnp.zeros_like(nodes[0]),) * 3
            else:
                total = tuple(start_ref[k, spans, rows, lanes] for k in range(3))
            total = add_points(table, number // BATCH, nodes, total)
            for k in range(3):
                out_ref[k, spans, rows, lanes] = total[k]
        return carry

    lax.fori_loop(0, 8, part, 0)


def flags(mask):
    return jnp.where(mask, 1.0, 0.0).astype(jnp.bfloat16)


def build_lists(values, useds, drops, boxes, z_low, z_high, kept):
    groups, depth = len(values), z_low.shape[1]
    row_at = lax.broadcasted_iota(jnp.int32, (8, 128), 0)
    big_lane = lax.broadcasted_iota(jnp.int32, (128, 128), 1)
    big_row = lax.broadcasted_iota(jnp.int32, (128, 128), 0)
    blank = jnp.zeros((4, 128), jnp.float32)
    keys, keeps, reaches = [], [], []
    for value, used, drop in zip(values, useds, drops):
        keys.append(value[2:3])
        apart = []
        for axis in range(2):
            along = value[axis : axis + 1]
            gaps = [jnp.maximum(jnp.maximum(b[0] - along, along - b[1]), 0.0) for b in boxes[axis]]
            apart.append([gap * gap for gap in gaps])
        spare = [REACH * REACH - apart[0][h] - apart[1][c] for h in range(2) for c in range(2)]
        spare = jnp.concatenate(spare + [blank], axis=0)
        near = (spare > 0.0) & used & (row_at < 4)
        keep = jnp.where(near, 1.0, 0.0)
        if drop is not None:
            keep = jnp.where(drop > 0.5, 0.0, keep)
        keeps.append(keep)
        reaches.append(jnp.where(near, jnp.sqrt(jnp.maximum(spare, 0.0)) * 1.01 + 0.01, 0.0))
    doubled = [jnp.concatenate([k, jnp.zeros_like(k)], axis=0).astype(jnp.bfloat16) for k in keeps]

    columns = [jnp.broadcast_to(key, (128, 128)).T for key in keys]

    def counted(blocks):
        return sum(
            jnp.dot(keep, block, preferred_element_type=jnp.float32)
            for keep, block in zip(doubled, blocks)
        )

    ahead = []
    for j in range(groups):
        row = []
        for i in range(groups):
            if j < i:
                before = columns[j] <= keys[i]
            elif j > i:
                before = columns[j] < keys[i]
            else:
                before = (columns[j] < keys[i]) | ((columns[j] == keys[i]) & (big_row < big_lane))
            row.append(flags(before))
        ahead.append(jnp.concatenate(row, axis=1))
    rank = counted(ahead)
    wide = [jnp.concatenate([c] * (depth // 128), axis=1) for c in columns]
    first = counted([flags(c < z_low - REACH) for c in wide])
    final = counted([flags(c <= z_high + REACH) for c in wide])

    parts = []
    for value, reach in zip(values, reaches):
        one = value.astype(jnp.bfloat16).astype(jnp.float32)
        rest = value - one
        two = rest.astype(jnp.bfloat16).astype(jnp.float32)
        three = rest - two
        parts.append(jnp.concatenate([one, two, three, reach], axis=0).astype(jnp.bfloat16))
    order = big_row.astype(jnp.float32)
    step_at = lax.broadcasted_iota(jnp.int32, (kept, depth), 0)
    lower = lax.broadcasted_iota(jnp.int32, (kept, kept), 0) > lax.broadcasted_iota(
        jnp.int32, (kept, kept), 1
    )
    lists = []
    for g in range(4):
        total = jnp.zeros((32, 128 * groups), jnp.float32)
        for i in range(groups):
            keep = keeps[i][g : g + 1] > 0.5
            at = jnp.where(keep, rank[g : g + 1, 128 * i : 128 * i + 128], -1.0)
            place = jnp.concatenate([flags(at == order + 128.0 * j) for j in range(groups)], axis=0)
            total = total + lax.dot_general(
                parts[i], place, (((1,), (1,)), ((), ())), preferred_element_type=jnp.float32
            )
        listed = total[0:8] + total[8:16] + total[16:24]
        start = first[g : g + 1].astype(jnp.int32)
        index = step_at + start
        bound = final[g : g + 1].astype(jnp.int32)

        def looked(row):
            tiles = [jnp.broadcast_to(row[:, 128 * j : 128 * j + 128], (8, 128)) for j in range(groups)]
            rows = []
            for k in range(kept // 8):
                cols = []
                for h in range(depth // 128):
                    want = index[8 * k : 8 * k + 8, 128 * h : 128 * h + 128]
                    found = jnp.zeros((8, 128), jnp.float32)
                    for j, tile in enumerate(tiles):
                        more = jnp.take_along_axis(tile, want & 127, axis=1)
                        found = jnp.where(want >> 7 == j, more, found)
                    cols.append(found)
                rows.append(jnp.concatenate(cols, axis=1))
            return jnp.concatenate(rows, axis=0)

        z = looked(listed[2:3])
        reach = looked(total[24 + g : 25 + g])
        inside = (index < bound) & (z > z_low - reach) & (z < z_high + reach)
        skipped = jnp.dot(
            flags(lower), flags(jnp.logical_not(inside)), preferred_element_type=jnp.float32
        )
        code = jnp.where(inside, index * 64 + skipped.astype(jnp.int32), NOWHERE)
        shift = 1
        while shift < kept:
            later = pltpu.roll(code, kept - shift, axis=0)
            left = jnp.where((code & shift) != 0, NOWHERE, code)
            code = jnp.where(((later & shift) != 0) & (step_at < kept - shift), later, left)
            shift = 2 * shift
        number = jnp.sum(jnp.where(inside, 1, 0), axis=0, keepdims=True)
        lists.append((listed, code >> 6, number, start, bound))
    return lists


def gather_kernel(
    x_hbm,
    q_hbm,
    points_hbm,
    coef_hbm,
    tiles_hbm,
    count_ref,
    x_v,
    q_v,
    sorted_ref,
    index_ref,
    first_ref,
    limits_ref,
    part_ref,
    rims_ref,
    tile_v,
    own,
    window,
    stage,
    table,
    own_sorted,
    own_index,
    fits_ref,
    tiles_ref,
    local_sems,
    send_sems,
    recv_sems,
):
    window[...] = jnp.zeros_like(window)
    wait_all = meet(AROUND)
    fetches = []
    for src, dst in (
        (points_hbm, tile_v.at[0]),
        (coef_hbm, tile_v.at[1]),
        (tiles_hbm, tiles_ref),
        (x_hbm, x_v),
        (q_hbm, q_v),
    ):
        fetch = pltpu.make_async_copy(src, dst, local_sems.at[len(fetches)])
        fetch.start()
        fetches.append(fetch)
    fetches[0].wait()
    fetches[1].wait()

    scale = 1.0 / RADIUS
    own[...] = jnp.zeros_like(own)
    for half in range(2):
        lanes = pl.ds(64 * half, 64)
        own[0:3, lanes] = tile_v[0, :, 0, :] * scale
        own[3:6, lanes] = tile_v[1, :, 0, :] * 4.0

    length = x_v.shape[1]
    span_at, chord_at = lax.axis_index("span"), lax.axis_index("chord")
    chords = lax.axis_size("chord")
    lane = lax.broadcasted_iota(jnp.int32, (8, 128), 1)
    row_at = lax.broadcasted_iota(jnp.int32, (8, 128), 0)

    def prepare():
        for fetch in fetches[2:]:
            fetch.wait()
        for side, row in ((2, 0), (3, length - 1)):
            stage[side, 0:3] = x_v[:, :, row, :]
            stage[side, 3:8] = q_v[:, :, row, :]
        for side, row in ((0, 0), (1, length - 1)):
            stage[side, 0:3] = x_v[:, row]
            stage[side, 3:8] = q_v[:, row]

    def bounds(block):
        low = jnp.min(jnp.min(block, axis=0), axis=0, keepdims=True) * scale
        high = jnp.max(jnp.max(block, axis=0), axis=0, keepdims=True) * scale
        return low, high

    def interval(block):
        low, high = bounds(block)
        return jnp.min(low, axis=1, keepdims=True), jnp.max(high, axis=1, keepdims=True)

    def all_bounds():
        boxes = (
            [interval(x_v[0, 8 * h : 8 * h + 8]) for h in range(2)],
            [interval(x_v[1, :, 8 * c : 8 * c + 8]) for c in range(2)],
        )
        return boxes, *bounds(x_v[2])

    def place_of(slot):
        tile = tiles_ref[0, 0, slot]
        at = (tile // chords - span_at + 1) * 3 + (tile % chords - chord_at + 1)
        return jnp.where(slot < count_ref[0, 0], jnp.clip(at, 0, 8), 9)

    def take_own():
        own_used = sum(jnp.where(place_of(slot) == 4, 1, 0) for slot in range(SLOTS)) > 0
        lists = build_lists([own[...]], [lane < 64], [None], *all_bounds(), OWN_KEPT)
        fits = []
        for g, (listed, index, number, start, bound) in enumerate(lists):
            own_sorted[g] = listed
            fit = (jnp.max(number, axis=1, keepdims=True) <= OWN) & (
                jnp.max(bound - start, axis=1, keepdims=True) <= OWN_KEPT
            )
            own_index[g] = jnp.where(fit & own_used, index, NOWHERE >> 6)
            fits.append(jnp.broadcast_to(jnp.where(fit, 1.0, 0.0), (1, 128)))
        fits_ref[...] = jnp.concatenate(fits + [jnp.zeros((4, 128), jnp.float32)], axis=0)
        add_listed(own_sorted, own_index, table, x_v, None, part_ref, OWN)

    ahead = lax.rem(chord_at, 4) < 2

    @pl.when(ahead)
    def _():
        prepare()
        take_own()

    wait_all()

    copies = []

    def remote(src, dst, offset):
        at = len(copies)
        copy = pltpu.make_async_remote_copy(
            src_ref=src,
            dst_ref=dst,
            send_sem=send_sems.at[at],
            recv_sem=recv_sems.at[at],
            device_id=peer(offset),
            device_id_type=MESH,
        )
        copies.append((copy, offset))

    for a, b in AROUND:
        remote(own, window.at[(1 - a) * 3 + 1 - b], (a, b))
        pl.when(exists((a, b)))(copies[-1][0].start)
    window[4] = own[...]
    pl.when(jnp.logical_not(ahead))(prepare)
    for side, offset in enumerate(SIDES):
        remote(stage.at[side], rims_ref.at[side ^ 1], offset)
    start_far_first(copies[8:])
    pl.when(jnp.logical_not(ahead))(take_own)
    boxes, z_low, z_high = all_bounds()
    places = [place_of(slot) for slot in range(SLOTS)]
    fits = fits_ref[...]

    wait_for(copies[:8])
    values, useds, drops = [], [], []
    for pair in range(SLOTS // 2):
        left, right = places[2 * pair], places[2 * pair + 1]
        value = jnp.where(
            lane < 64, window[jnp.where(left > 8, 4, left)], window[jnp.where(right > 8, 4, right)]
        )
        place = jnp.where(lane < 64, left, right)
        useds.append(place <= 8)
        drops.append(jnp.where(place == 4, fits, 0.0))
        values.append(jnp.where((row_at >= 3) & (place > 8), 0.0, value))
    lists = build_lists(values, useds, drops, boxes, z_low, z_high, KEPT)
    limits = jnp.zeros((8, 128), jnp.int32)
    for g, (listed, index, number, start, bound) in enumerate(lists):
        sorted_ref[g] = listed
        first_ref[g] = jnp.broadcast_to(start, first_ref.shape[1:])
        for h in range(index.shape[1] // 128):
            cut = slice(128 * h, 128 * h + 128)
            most = jnp.max((bound - start)[:, cut], axis=1, keepdims=True)
            index_ref[g, :, cut] = jnp.where(most <= KEPT, index[:, cut], NOWHERE >> 6)
            found = (
                jnp.max(number[:, cut], axis=1, keepdims=True),
                most,
                jnp.max(bound[:, cut], axis=1, keepdims=True),
            )
            for i, limit in enumerate(found):
                limits = jnp.where((row_at == g) & (lane == 3 * h + i), limit, limits)
    limits_ref[...] = limits
    add_listed(sorted_ref, index_ref, table, x_v, part_ref, part_ref, EARLY)
    wait_for(copies[8:])


def gather(node_coords, primitives, control_points, coefficients, tiles, counts):
    depth = node_coords.shape[3]
    vmem = pl.BlockSpec(memory_space=pltpu.VMEM)
    hbm = pl.BlockSpec(memory_space=pltpu.HBM)
    f32 = jnp.float32
    return pl.pallas_call(
        gather_kernel,
        out_shape=(
            jax.ShapeDtypeStruct(node_coords.shape, f32),
            jax.ShapeDtypeStruct(primitives.shape, f32),
            jax.ShapeDtypeStruct((4, 8, 64 * SLOTS), f32),
            jax.ShapeDtypeStruct((4, KEPT, depth), jnp.int32),
            jax.ShapeDtypeStruct((4, 8, depth), jnp.int32),
            jax.ShapeDtypeStruct((8, 128), jnp.int32),
            jax.ShapeDtypeStruct(node_coords.shape, f32),
            jax.ShapeDtypeStruct((4, 8, 16, depth), f32),
        ),
        in_specs=[hbm] * 5 + [pl.BlockSpec(memory_space=pltpu.SMEM)],
        out_specs=(vmem,) * 8,
        scratch_shapes=[
            pltpu.VMEM((2,) + control_points.shape, f32),
            pltpu.VMEM((8, 128), f32),
            pltpu.VMEM((9, 8, 128), f32),
            pltpu.VMEM((4, 8, 16, depth), f32),
            pltpu.VMEM((OWN_KEPT, 8, 128), f32),
            pltpu.VMEM((4, 8, 128), f32),
            pltpu.VMEM((4, OWN_KEPT, depth), jnp.int32),
            pltpu.VMEM((8, 128), f32),
            pltpu.SMEM(tiles.shape, jnp.int32),
            pltpu.SemaphoreType.DMA((5,)),
            pltpu.SemaphoreType.DMA((12,)),
            pltpu.SemaphoreType.DMA((12,)),
        ],
        compiler_params=pltpu.CompilerParams(
            collective_id=0, has_side_effects=True, vmem_limit_bytes=32 << 20
        ),
        name="gather",
    )(
        *(
            pltpu.with_memory_space_constraint(v, pltpu.HBM)
            for v in (node_coords, primitives, control_points, coefficients, tiles)
        ),
        counts,
    )


SPANS_EACH = 4


def motion_kernel(limits_ref, sorted_ref, index_ref, first_ref, x_ref, begun_ref, m_ref, table):
    scale = 1.0 / RADIUS
    tiles = sorted_ref.shape[2] // 128

    def part(at, carry):
        g, half, lanes, rows, pieces = part_of(at)
        number, most, top = (limits_ref[g, 3 * half + k] for k in range(3))
        few = most <= KEPT
        number = jnp.where(few, jnp.maximum(number - EARLY, 0), most)

        def fill(tiles):
            def some(i, carry):
                start = pl.multiple_of(EARLY + i * 8, 8)
                batch = index_ref[g, pl.ds(start, 8), lanes]
                for u in range(8):
                    index = jnp.broadcast_to(batch[u : u + 1], (8, 128))
                    table[i * 8 + u] = look_up(sorted_ref, g, index, tiles)
                return carry

            lax.fori_loop(0, (number + 7) // 8, some, 0)

        @pl.when(few & (top <= 128))
        def _():
            fill(1)

        @pl.when(few & (top > 128))
        def _():
            fill(tiles)

        @pl.when(most > KEPT)
        def _():
            first = first_ref[g, :, lanes]

            def some(i, carry):
                for u in range(BATCH):
                    at = i * BATCH + u
                    table[at] = look_up(sorted_ref, g, first + at, tiles)
                return carry

            lax.fori_loop(0, (number + BATCH - 1) // BATCH, some, 0)

        @pl.when(number > 0)
        def _():
            for spans in pieces:
                nodes = [x_ref[k, spans, rows, lanes] * scale for k in range(3)]
                total = tuple(m_ref[k, spans, rows, lanes] for k in range(3))
                total = add_points(table, (number + BATCH - 1) // BATCH, nodes, total)
                for k in range(3):
                    m_ref[k, spans, rows, lanes] = total[k]

        return carry

    lax.fori_loop(0, 8, part, 0)


def motion(limits, points, index, first, coords, begun):
    vmem = pl.BlockSpec(memory_space=pltpu.VMEM)
    smem = pl.BlockSpec(memory_space=pltpu.SMEM)
    return pl.pallas_call(
        motion_kernel,
        out_shape=jax.ShapeDtypeStruct(coords.shape, jnp.float32),
        in_specs=[smem] + [vmem] * 5,
        out_specs=vmem,
        scratch_shapes=[pltpu.VMEM((64 * SLOTS + 8, 8, 128), jnp.float32)],
        input_output_aliases={5: 0},
        compiler_params=pltpu.CompilerParams(vmem_limit_bytes=32 << 20),
        name="motion",
    )(limits, points, index, first, coords, begun)


def node_fields(coords, speed, state):
    rho, u, p = state[0], state[1:4], state[4]
    kinetic = 0.5 * rho * (u[0] * u[0] + u[1] * u[1] + u[2] * u[2])
    return dict(
        place=[a + b for a, b in zip(coords, speed)],
        speed=speed,
        u=u,
        p=p,
        amounts=[rho] + [rho * v for v in u] + [p / (GAMMA_GAS - 1.0) + kinetic],
        sound=jnp.sqrt(GAMMA_GAS * p / rho),
    )


def dot3(a, b):
    return a[0] * b[0] + a[1] * b[1] + a[2] * b[2]


def double_flux(left, right):
    edge = [b - a for a, b in zip(left["place"], right["place"])]
    magnitude = lax.rsqrt(dot3(edge, edge))
    inverse = magnitude * magnitude
    normal = [e * inverse for e in edge]
    frame = 0.5 * dot3([a + b for a, b in zip(left["speed"], right["speed"])], normal)
    left_un, right_un = dot3(left["u"], normal), dot3(right["u"], normal)
    left_rel, right_rel = left_un - frame, right_un - frame
    signal = jnp.maximum(
        jnp.abs(left_rel) + left["sound"] * magnitude,
        jnp.abs(right_rel) + right["sound"] * magnitude,
    )
    left_gain, right_gain = left_rel + signal, right_rel - signal
    flux = [a * left_gain + b * right_gain for a, b in zip(left["amounts"], right["amounts"])]
    pressure = left["p"] + right["p"]
    for k in range(3):
        flux[1 + k] = flux[1 + k] + pressure * normal[k]
    flux[4] = flux[4] + left["p"] * left_un + right["p"] * right_un
    return flux


def flux_kernel(
    x_ref,
    m_ref,
    q_ref,
    out_ref,
    landed,
    stage,
    send_sems,
    recv_sems,
):
    wait_all = meet(SIDES)
    length, chord_len, depth = x_ref.shape[1:]
    last = length - 1
    stage[0] = m_ref[:, 0]
    stage[1] = m_ref[:, last]
    stage[2] = m_ref[:, :, 0, :]
    stage[3] = m_ref[:, :, last, :]
    copies = []
    for side, offset in enumerate(SIDES):
        copy = pltpu.make_async_remote_copy(
            src_ref=stage.at[side],
            dst_ref=landed.at[side ^ 1],
            send_sem=send_sems.at[side],
            recv_sem=recv_sems.at[side ^ 1],
            device_id=peer(offset),
            device_id_type=MESH,
        )
        copies.append((copy, offset))

    step = 0.5 * SECTION_BETA

    def plane(s):
        return node_fields(
            [x_ref[k, s] for k in range(3)],
            [m_ref[k, s] for k in range(3)],
            [q_ref[k, s] for k in range(5)],
        )

    def moved(fields, axis):
        size = (chord_len, depth)[axis]

        def roll(v):
            return pltpu.roll(v, size - 1, axis=axis)

        return {
            name: [roll(v) for v in value] if isinstance(value, (list, tuple)) else roll(value)
            for name, value in fields.items()
        }

    row_at = lax.broadcasted_iota(jnp.int32, (chord_len, depth), 0)
    lane_at = lax.broadcasted_iota(jnp.int32, (chord_len, depth), 1)

    def inner(s, before):
        here = plane(s)
        ahead = plane(jnp.minimum(s + 1, last))
        span = double_flux(here, ahead)
        span = [jnp.where(s < last, f, 0.0) for f in span]
        chord = double_flux(here, moved(here, 0))
        chord = [jnp.where(row_at < chord_len - 1, f, 0.0) for f in chord]
        normal = double_flux(here, moved(here, 1))
        normal = [jnp.where(lane_at < depth - 1, f, 0.0) for f in normal]
        for k in range(5):
            residual = span[k] - before[k]
            residual = residual + (chord[k] - pltpu.roll(chord[k], 1, axis=0))
            residual = residual + (normal[k] - pltpu.roll(normal[k], 1, axis=1))
            out_ref[k, s] = here["amounts"][k] - step * residual
        return tuple(span)

    zero = jnp.zeros((chord_len, depth), jnp.float32)
    before = lax.fori_loop(0, AHEAD, inner, (zero,) * 5)
    wait_all()
    start_far_first(copies)
    lax.fori_loop(AHEAD, length, inner, before)
    wait_for(copies)


def section(node_coords, moved, primitives):
    depth = node_coords.shape[3]
    vmem = pl.BlockSpec(memory_space=pltpu.VMEM)
    f32 = jnp.float32
    return pl.pallas_call(
        flux_kernel,
        out_shape=(
            jax.ShapeDtypeStruct(primitives.shape, f32),
            jax.ShapeDtypeStruct((4, 3, 16, depth), f32),
        ),
        in_specs=[vmem] * 3,
        out_specs=(vmem,) * 2,
        scratch_shapes=[
            pltpu.VMEM((4, 3, 16, depth), f32),
            pltpu.SemaphoreType.DMA((4,)),
            pltpu.SemaphoreType.DMA((4,)),
        ],
        compiler_params=pltpu.CompilerParams(
            collective_id=1, has_side_effects=True, vmem_limit_bytes=32 << 20
        ),
        name="section",
    )(node_coords, moved, primitives)


def finish_kernel(
    x_ref, m_ref, q_ref, rims_ref, landed_ref, inner_ref, motion_hbm, state_hbm, rim_flux, out, sems
):
    length, chord_len, depth = x_ref.shape[1:]
    last = length - 1
    step = 0.5 * SECTION_BETA
    send_motion = pltpu.make_async_copy(m_ref, motion_hbm, sems.at[0])
    send_motion.start()

    def add_side(side):
        row = last * (side % 2)
        sign = step if side % 2 == 0 else -step

        @pl.when(exists(SIDES[side]))
        def _():
            def rim(ref, k):
                return ref[k, row] if side < 2 else ref[k, :, row, :]

            here = node_fields(
                [rim(x_ref, k) for k in range(3)],
                [rim(m_ref, k) for k in range(3)],
                [rim(q_ref, k) for k in range(5)],
            )
            there = node_fields(
                [rims_ref[side, k] for k in range(3)],
                [landed_ref[side, k] for k in range(3)],
                [rims_ref[side, 3 + k] for k in range(5)],
            )
            flux = double_flux(there, here) if side % 2 == 0 else double_flux(here, there)
            for k in range(5):
                rim_flux[side, k] = sign * flux[k]

        @pl.when(jnp.logical_not(exists(SIDES[side])))
        def _():
            rim_flux[side] = jnp.zeros(rim_flux.shape[1:], jnp.float32)

    row_at = lax.broadcasted_iota(jnp.int32, (chord_len, depth), 0)
    sends = [send_motion]

    def with_rows(k, s):
        low = jnp.where(row_at == 0, rim_flux[2, k, s : s + 1], 0.0)
        return inner_ref[k, s] + jnp.where(row_at == last, rim_flux[3, k, s : s + 1], low)

    def give(part):
        sends.append(pltpu.make_async_copy(out.at[part], state_hbm.at[part], sems.at[len(sends)]))
        sends[-1].start()

    add_side(2)
    add_side(3)
    for k in range(5):
        for s in range(1, last):
            out[k, s] = with_rows(k, s)
        give((k, pl.ds(1, last - 1)))
    for side, s in ((0, 0), (1, last)):
        add_side(side)
        for k in range(5):
            out[k, s] = with_rows(k, s) + rim_flux[side, k]
        give((slice(None), s))
    for sent in sends:
        sent.wait()


def finish(coords, moved, states, rims, landed, inner):
    vmem = pl.BlockSpec(memory_space=pltpu.VMEM)
    hbm = pl.BlockSpec(memory_space=pltpu.HBM)
    f32 = jnp.float32
    return pl.pallas_call(
        finish_kernel,
        out_shape=(pltpu.HBM(moved.shape, f32), pltpu.HBM(states.shape, f32)),
        in_specs=[vmem] * 6,
        out_specs=(hbm, hbm),
        scratch_shapes=[
            pltpu.VMEM((4, 5, 16, coords.shape[3]), f32),
            pltpu.VMEM(states.shape, f32),
            pltpu.SemaphoreType.DMA((8,)),
        ],
        compiler_params=pltpu.CompilerParams(vmem_limit_bytes=32 << 20),
        name="finish",
    )(coords, moved, states, rims, landed, inner)


def body(node_coords, primitives, control_points, coefficients, support_tiles, support_counts):
    coords, states, points, index, first, limits, begun, rims = gather(
        node_coords, primitives, control_points, coefficients, support_tiles, support_counts
    )
    moved = motion(limits, points, index, first, coords, begun)
    inner, landed = section(coords, moved, states)
    return finish(coords, moved, states, rims, landed, inner)


def solution(mesh):
    in_specs = (
        P(None, "span", "chord", None),
        P(None, "span", "chord", None),
        P(None, ("span", "chord"), None),
        P(None, ("span", "chord"), None),
        P("span", "chord", None),
        P("span", "chord"),
    )
    out_specs = (P(None, "span", "chord", None), P(None, "span", "chord", None))
    return jax.shard_map(body, mesh=mesh, in_specs=in_specs, out_specs=out_specs, check_vma=False)
```
